512 devices in a mesh: lon: 32 (over x_lo, z), lat: 16 (over x_hi, y, core).
Axes of the slice: x: 4 (x_hi: 2, x_lo: 2; x = x_hi * 2 + x_lo), y: 4, z: 16, core: 2. Of those that a mesh axis runs over, the one named last changes fastest.
Arguments:
- tokens: bfloat16 [2, 384, 384, 192], P(None, 'lat', 'lon'), may hold values from -6 to 6
- cotangent: bfloat16 [2, 384, 384, 192], P(None, 'lat', 'lon'), may hold values from -6 to 6
- w_qkv: bfloat16 [192, 576], replicated, may hold values from -0.4375 to 0.4375
- w_proj: bfloat16 [192, 192], replicated, may hold values from -0.4375 to 0.4375
- w_up: bfloat16 [192, 768], replicated, may hold values from -0.4375 to 0.4375
- w_down: bfloat16 [768, 192], replicated, may hold values from -0.21875 to 0.21875
- bias_table: bfloat16 [32, 19872], replicated, may hold values from -4 to 220
- band_rows: int32 [16], replicated, may hold values from 1 to 4, 32 in all
- lon_shift: int32 [32], replicated, may hold values from 1 to 11
Outputs:
- output: bfloat16 [2, 384, 384, 192], P(None, 'lat', 'lon')
- grad_tokens: bfloat16 [2, 384, 384, 192], P(None, 'lat', 'lon')
- grad_qkv: float32 [192, 576], P('lat', 'lon')
- grad_proj: float32 [192, 192], P('lat', 'lon')
- grad_up: float32 [192, 768], P('lat', 'lon')
- grad_down: float32 [768, 192], P('lat', 'lon')
- grad_table: float32 [32, 19872], P('lat', 'lon')
The draws below stay inside these ranges and needn't reach their ends.
Inputs may be any that keep to these rules, and one draw needn't show every extreme that they name: Band b holds its rows in its first band_rows[b] slots; the entries sum to 32 and the largest is exactly 4.
All inputs are finite; a program needn't handle non-finite values.
Results may differ from the reference program's by a relative error of at most 0.04.
Values may be sent and summed in bfloat16 or wider, within the bound.
No kernel may reach another device: no remote copies, remote signals or barrier semaphores. Data moves between devices by JAX's collectives and lax.ppermute only.
A program may use at most 192 MiB of HBM per device.

```python
import math
import jax
import jax.numpy as jnp
import numpy as np
from jax import lax

D = 192
HEADS = 6
HID = 768
WZ = 2
WH = 6
WW = 12
LEVELS = 2
RMAX = 4
LATWIN = 32
WTOK = 144
POS = 3312
NLAT_CELLS = 384
NLON_CELLS = 384
CELLS = 147456
N_LAT = 16


def draw_bias_table(key, part):
    key = jax.random.fold_in(key, 7)
    base_key = jax.random.fold_in(key, 0)
    table_shape = (LATWIN, HEADS, POS)
    bias_vals = jnp.clip(jax.random.normal(base_key, table_shape, jnp.float32), -4.0, 4.0)
    return bias_vals.reshape(LATWIN, HEADS * POS).astype(jnp.bfloat16)


def plant(result, own_key, smallest, largest):
    spot = [jax.random.randint(jax.random.fold_in(own_key, axis), (), 0, length) for axis, length in enumerate(result.shape)]
    widest = result.shape.index(max(result.shape))
    next_to = spot[:widest] + [(spot[widest] + 1) % result.shape[widest]] + spot[widest + 1:]
    return result.at[tuple(spot)].set(smallest).at[tuple(next_to)].set(largest)


def steps_of(rng, shape, cuts, least, top_value):
    loudness = 1.0
    for dim, shards_of in cuts:
        heights = jax.random.uniform(jax.random.fold_in(jax.random.fold_in(rng, 6), dim), (shards_of,), jnp.float32, least / len(cuts), top_value / len(cuts))
        loudness = loudness * jnp.repeat(jnp.exp(heights), shape[dim] // shards_of).reshape((-1,) + (1,) * (len(shape) - 1 - dim))
    return loudness


def split_up(number_of, total, limit, skew):
    loads = [(1 << 20) // math.isqrt(grade ** skew) + 1 for grade in range(2, number_of + 1)]
    surplus, given = total - limit - (number_of - 1), [1] * (number_of - 1)
    while surplus > 0:
        candidates = [i for i in range(number_of - 1) if given[i] < limit]
        whole, remaining = sum([loads[i] for i in candidates]), surplus
        for i in candidates:
            extra = min(limit - given[i], max(1, remaining * loads[i] // whole), surplus)
            given[i] = given[i] + extra
            surplus = surplus - extra
    return np.array([limit] + given)


def ragged(rng, amount, total, reach, lean):
    if amount == 2:
        one = jax.random.randint(rng, (), max(1, total - reach), min(reach, total - 1) + 1)
        return jnp.stack([one, total - one])
    tallies = jnp.asarray(split_up(amount, total, reach, lean), jnp.int32)
    couples = (amount - 1) // 2
    giver, taker = tallies[1:1 + 2 * couples:2], tallies[2:2 + 2 * couples:2]
    margin = jnp.minimum(giver - 1, reach - taker)
    passed = jax.random.randint(jax.random.fold_in(rng, 1), (couples,), 0, 1 << 20) % (margin + 1)
    tallies = tallies.at[1:1 + 2 * couples:2].set(giver - passed).at[2:2 + 2 * couples:2].set(taker + passed)
    return tallies[jax.random.permutation(jax.random.fold_in(rng, 2), amount)]


def gaussian(rng, extent, spread, most, cuts=(), kind=jnp.bfloat16):
    array = jax.random.normal(rng, extent, jnp.float32) * spread
    if len(cuts) > 0:
        array = steps_of(rng, extent, cuts, -0.22, 0.18) * array
    return jnp.clip(array, min=-most, max=most).astype(kind)


def setup_inputs(seed: int = 0) -> dict:
    splits = jax.random.split(jax.random.key(seed), 10)
    return {
        "tokens": gaussian(splits[0], (LEVELS, NLAT_CELLS, NLON_CELLS, D), 1.0, 6.0, ((1, 16), (2, 32))),
        "cotangent": gaussian(splits[1], (LEVELS, NLAT_CELLS, NLON_CELLS, D), 1.0, 6.0, ((1, 16), (2, 32))),
        "w_qkv": gaussian(splits[2], (D, 3 * D), D ** -0.5, 0.4375),
        "w_proj": gaussian(splits[3], (D, D), D ** -0.5, 0.4375),
        "w_up": gaussian(splits[4], (D, HID), D ** -0.5, 0.4375),
        "w_down": gaussian(splits[5], (HID, D), HID ** -0.5, 0.21875),
        "bias_table": draw_bias_table(jax.random.fold_in(splits[9], 71), 0),
        "band_rows": ragged(splits[7], N_LAT, LATWIN, RMAX, 2).astype(jnp.int32),
        "lon_shift": plant(jax.random.randint(splits[8], (LATWIN,), 1, WW), jax.random.fold_in(splits[8], 1), 1, WW - 1).astype(jnp.int32),
    }


epsilon = 1e-05

def product(form, left, right):
    return jnp.einsum(form, left.astype(jnp.float32), right.astype(jnp.float32))

def position_index():
    rel_span = 2 * WW - 1
    cell_ids = jnp.arange(WTOK, dtype=jnp.int32)
    level_pos = cell_ids // (WH * WW)
    row_pos = cell_ids // WW % WH
    column_pos = cell_ids % WW
    pos_flat = (level_pos[:, None] + level_pos[None, :] * WZ) * (WH * WH * rel_span)
    pos_flat = pos_flat + (row_pos[:, None] + row_pos[None, :] * WH) * rel_span
    pos_flat = pos_flat + column_pos[:, None] - column_pos[None, :] + WW - 1
    return pos_flat.reshape(-1).astype(jnp.int32)

def make_bias(table_rows, pos_flat):
    n_rows = table_rows.shape[0]
    shaped = table_rows.reshape(n_rows, HEADS, POS)
    picked = jnp.take(shaped, pos_flat, axis=2)
    return picked.reshape(n_rows, HEADS, WTOK, WTOK).astype(jnp.float32)

def table_grad(grad_bias, pos_flat):
    n_rows = grad_bias.shape[0]
    flat_grad = grad_bias.reshape(n_rows * HEADS, WTOK * WTOK).T
    summed = jax.ops.segment_sum(flat_grad, pos_flat, num_segments=POS)
    return summed.T.reshape(n_rows, HEADS * POS)

def to_windows(grid, n_rows, n_win):
    model_width = grid.shape[-1]
    parted = grid.reshape(LEVELS, n_rows, WH, n_win, WW, model_width)
    return parted.transpose(1, 3, 0, 2, 4, 5).reshape(n_rows, n_win, WTOK, model_width)

def from_windows(blocks):
    n_rows = blocks.shape[0]
    n_win = blocks.shape[1]
    model_width = blocks.shape[3]
    parted = blocks.reshape(n_rows, n_win, LEVELS, WH, WW, model_width)
    return parted.transpose(2, 0, 3, 1, 4, 5).reshape(LEVELS, n_rows * WH, n_win * WW, model_width)

def normalize(values):
    centre = lax.optimization_barrier(jnp.mean(values, axis=-1, keepdims=True))
    shifted = values - centre
    inv_std = lax.rsqrt(lax.optimization_barrier(jnp.mean(shifted * shifted, axis=-1, keepdims=True)) + epsilon)
    return (shifted * inv_std, inv_std)

def norm_back(normed, inv_std, grad_normed):
    mean_grad = lax.optimization_barrier(jnp.mean(grad_normed, axis=-1, keepdims=True))
    mean_proj = lax.optimization_barrier(jnp.mean(grad_normed * normed, axis=-1, keepdims=True))
    return inv_std * (grad_normed - mean_grad - normed * mean_proj)

def gelu_parts(pre_act):
    gauss_cdf = 0.5 * (1.0 + lax.erf(pre_act * 0.7071067811865476))
    density = jnp.exp(-0.5 * pre_act * pre_act) * 0.3989422804014327
    return (pre_act * gauss_cdf, gauss_cdf + pre_act * density)

def window_pass(windows, cotan, bias, keep_mask, w_qkv, w_proj, w_up, w_down):
    n_rows, n_win, n_tok, model_width = windows.shape
    n_heads = bias.shape[1]
    head_dim = model_width // n_heads
    q_scale = head_dim ** (-0.5)
    head_shape = (n_rows, n_win, n_tok, n_heads, head_dim)
    tokens_f = windows.astype(jnp.float32)
    normed_a, inv_a = normalize(tokens_f)
    normed_a_b = normed_a.astype(jnp.bfloat16)
    qkv_all = product('rntd,de->rnte', normed_a_b, w_qkv)
    query = (qkv_all[..., :model_width] * q_scale).astype(jnp.bfloat16).reshape(head_shape)
    key_cells = qkv_all[..., model_width:2 * model_width].astype(jnp.bfloat16).reshape(head_shape)
    values = qkv_all[..., 2 * model_width:].astype(jnp.bfloat16).reshape(head_shape)
    scores = product('rnqhc,rnkhc->rnhqk', query, key_cells) + bias[:, None]
    row_top = lax.optimization_barrier(jnp.max(scores, axis=-1, keepdims=True))
    exp_scores = jnp.exp(scores - row_top)
    probs_f = exp_scores / lax.optimization_barrier(jnp.sum(exp_scores, axis=-1, keepdims=True))
    probs_b = probs_f.astype(jnp.bfloat16)
    attended = product('rnhqk,rnkhc->rnqhc', probs_b, values)
    attended = attended.reshape(n_rows, n_win, n_tok, model_width).astype(jnp.bfloat16)
    hidden = tokens_f + product('rntd,de->rnte', attended, w_proj)
    normed_b, inv_b = normalize(hidden)
    normed_b_b = normed_b.astype(jnp.bfloat16)
    pre_act = product('rntd,df->rntf', normed_b_b, w_up)
    act_f, gelu_slope = gelu_parts(pre_act)
    act_b = act_f.astype(jnp.bfloat16)
    output = (hidden + product('rntf,fd->rntd', act_b, w_down)).astype(jnp.bfloat16)
    keep_b = keep_mask[:, :, None, None].astype(jnp.bfloat16)
    grad_down = product('rntf,rntd->fd', act_b * keep_b, cotan)
    grad_act = product('rntd,fd->rntf', cotan, w_down)
    grad_pre = (grad_act * gelu_slope).astype(jnp.bfloat16)
    grad_up = product('rntd,rntf->df', normed_b_b * keep_b, grad_pre)
    grad_normed = product('rntf,df->rntd', grad_pre, w_up)
    grad_hidden = cotan.astype(jnp.float32) + norm_back(normed_b, inv_b, grad_normed)
    grad_hidden_b = grad_hidden.astype(jnp.bfloat16)
    grad_proj = product('rnte,rntd->ed', attended * keep_b, grad_hidden_b)
    grad_att = product('rntd,ed->rnte', grad_hidden_b, w_proj).astype(jnp.bfloat16).reshape(head_shape)
    grad_probs = product('rnqhc,rnkhc->rnhqk', grad_att, values)
    grad_scores = probs_f * (grad_probs - lax.optimization_barrier(jnp.sum(probs_f * grad_probs, axis=-1, keepdims=True)))
    grad_bias = lax.optimization_barrier(jnp.sum(grad_scores * keep_mask[:, :, None, None, None], axis=1))
    grad_scores_b = grad_scores.astype(jnp.bfloat16)
    grad_query = product('rnhqk,rnkhc->rnqhc', grad_scores_b, key_cells) * q_scale
    grad_keys = product('rnhqk,rnqhc->rnkhc', grad_scores_b, query)
    grad_values = product('rnhqk,rnqhc->rnkhc', probs_b, grad_att)
    flat_shape = (n_rows, n_win, n_tok, model_width)
    grad_cells = jnp.concatenate([grad_query.reshape(flat_shape), grad_keys.reshape(flat_shape), grad_values.reshape(flat_shape)], axis=-1).astype(jnp.bfloat16)
    grad_qkv = product('rntd,rnte->de', normed_a_b * keep_b, grad_cells)
    grad_in = product('rnte,de->rntd', grad_cells, w_qkv)
    grad_tokens = (grad_hidden + norm_back(normed_a, inv_a, grad_in)).astype(jnp.bfloat16)
    return (output, grad_tokens, (grad_qkv, grad_proj, grad_up, grad_down), grad_bias)

def reference(tokens, cotangent, w_qkv, w_proj, w_up, w_down, bias_table, band_rows, lon_shift):
    band_ends = jnp.cumsum(band_rows).astype(jnp.int32)
    band_starts = (band_ends - band_rows).astype(jnp.int32)
    pos_flat = position_index()
    n_win = NLON_CELLS // WW

    def slot_of(row_id):
        band_num = jnp.sum((band_ends <= row_id).astype(jnp.int32)).astype(jnp.int32)
        return (band_num * RMAX + row_id - band_starts[band_num]).astype(jnp.int32)

    def one_row(totals, row_id):
        offset = lon_shift[row_id].astype(jnp.int32)
        first_cell = (slot_of(row_id) * WH).astype(jnp.int32)
        x_row = jnp.roll(lax.dynamic_slice_in_dim(tokens, first_cell, WH, 1), -offset, axis=2)
        dy_row = jnp.roll(lax.dynamic_slice_in_dim(cotangent, first_cell, WH, 1), -offset, axis=2)
        bias = make_bias(lax.dynamic_slice_in_dim(bias_table, row_id, 1, 0), pos_flat)
        keep_mask = jnp.ones((1, n_win), jnp.float32)
        out_win, grad_win, grad_sums, grad_bias = window_pass(to_windows(x_row, 1, n_win), to_windows(dy_row, 1, n_win), bias, keep_mask, w_qkv, w_proj, w_up, w_down)
        out_row = jnp.roll(from_windows(out_win), offset, axis=2)
        grad_row = jnp.roll(from_windows(grad_win), offset, axis=2)
        totals = tuple((acc_sum + new_sum for acc_sum, new_sum in zip(totals, grad_sums)))
        return (totals, (out_row, grad_row, table_grad(grad_bias, pos_flat)[0]))
    init_sums = (jnp.zeros(w_qkv.shape, jnp.float32), jnp.zeros(w_proj.shape, jnp.float32), jnp.zeros(w_up.shape, jnp.float32), jnp.zeros(w_down.shape, jnp.float32))
    row_list = jnp.arange(LATWIN, dtype=jnp.int32)
    totals, stacked = lax.scan(one_row, init_sums, row_list)
    out_rows, grad_rows, table_rows = stacked
    slot_ids = jax.vmap(slot_of)(row_list)
    cell_index = (slot_ids[:, None] * WH + jnp.arange(WH, dtype=jnp.int32)[None, :]).reshape(-1).astype(jnp.int32)

    def place(rows_data):
        moved = rows_data.transpose(1, 0, 2, 3, 4).reshape(LEVELS, LATWIN * WH, NLON_CELLS, D)
        return jnp.zeros(tokens.shape, jnp.bfloat16).at[:, cell_index].set(moved.astype(jnp.bfloat16))
    scale_grad = CELLS ** (-0.5)
    return (place(out_rows), place(grad_rows), totals[0] * scale_grad, totals[1] * scale_grad, totals[2] * scale_grad, totals[3] * scale_grad, table_rows)
```

```python
import functools

import jax
import jax.numpy as jnp
import numpy as np
from jax import lax
from jax.experimental import pallas as pl
from jax.experimental.pallas import tpu as pltpu
from jax.sharding import PartitionSpec as P

HEADS = 6
HEAD = 32
WIDTH = 192
HID = 768
WH = 6
WW = 12
LEVELS = 2
SLOTS = 4
WTOK = 144
CELL_ROWS = 72
POS = 3312
SPAN = 23
LEFT = 5
RIGHT = 6
LAT = 24
NLAT = 16
NLON = 32
ALL_Q = HEADS * WTOK
GROUP = 4
PARTS = WW // GROUP
LANES_V = 384

bf16 = jnp.bfloat16
f32 = jnp.float32
epsilon = 1e-05

NN = (((1,), (0,)), ((), ()))
NT = (((1,), (1,)), ((), ()))


def mm(left, right, dims=NN):
    return lax.dot_general(left, right, dims, preferred_element_type=f32)


def one_hot(condition):
    return jnp.where(condition, 1.0, 0.0).astype(bf16)


def eye(count):
    rows = lax.broadcasted_iota(jnp.int32, (count, count), 0)
    cols = lax.broadcasted_iota(jnp.int32, (count, count), 1)
    return one_hot(rows == cols)


def spread_table():
    table = np.zeros((PARTS, LANES_V, WTOK), np.float32)
    for part in range(PARTS):
        for level in range(LEVELS):
            for row in range(WH):
                for col in range(WW):
                    e = col - GROUP * part + WW - GROUP
                    table[part, (level * WH + row) * SPAN + e, level * 72 + col * WH + row] = 1
    return table


def regroup_table():
    table = np.zeros((288, 288), np.float32)
    for head_level in range(12):
        for step in range(GROUP):
            for row in range(WH):
                table[(head_level * GROUP + step) * WH + row, step * 72 + head_level * WH + row] = 1
    return table


def entry_table():
    table = np.zeros((288, 288), np.float32)
    for head in range(HEADS):
        for zk in range(LEVELS):
            for zq in range(LEVELS):
                for hk in range(WH):
                    for half in range(2):
                        entry = (((head * 2 + zk) * 2 + zq) * WH + hk) * 2 + half
                        chunk, place = entry // 9, entry % 9
                        source = (zq * 2 + half) * 72 + (head * 2 + zk) * WH + hk
                        table[place * NLON + chunk, source] = 1
    return table


def layer_norm(x):
    centre = jnp.sum(x, axis=0, keepdims=True) * (1.0 / WIDTH)
    shifted = x - centre
    var = jnp.sum(shifted * shifted, axis=0, keepdims=True) * (1.0 / WIDTH)
    inv = lax.rsqrt(var + epsilon)
    return shifted * inv, inv


def norm_back(normed, inv, grad):
    mean_grad = jnp.sum(grad, axis=0, keepdims=True) * (1.0 / WIDTH)
    mean_proj = jnp.sum(grad * normed, axis=0, keepdims=True) * (1.0 / WIDTH)
    return inv * (grad - mean_grad - normed * mean_proj)


def bias_kernel(rows_ref, spread_ref, regroup_ref, bias_ref):
    regroup = regroup_ref[...]
    for slot in range(SLOTS):
        rows = rows_ref[slot].astype(f32)
        rows = jnp.concatenate([rows, jnp.zeros((72, LANES_V - 276), f32)], axis=1)
        shifted = [
            rows if step == GROUP - 1 else pltpu.roll(rows, LANES_V - (GROUP - 1 - step), 1)
            for step in range(GROUP)
        ]
        stack = jnp.concatenate(shifted, axis=0).astype(bf16)
        left = mm(regroup, stack).astype(bf16)
        for part in range(PARTS):
            full = mm(left, spread_ref[part])
            for head in range(HEADS):
                for level in range(LEVELS):
                    at = (head * 2 + level) * 24
                    bias_ref[
                        slot,
                        level * 72 + part * 24 : level * 72 + part * 24 + 24,
                        head * WTOK : (head + 1) * WTOK,
                    ] = full[at : at + 24, :]


def diagonal(full):
    return jnp.concatenate(
        [
            full[h * HEAD : (h + 1) * HEAD, h * WTOK : (h + 1) * WTOK]
            for h in range(HEADS)
        ],
        axis=0,
    )


def main_kernel(
    at_ref,
    left_ref,
    own_t_ref,
    own_c_ref,
    right_ref,
    bias_ref,
    wqkv_ref,
    wqkv_t_ref,
    wproj_ref,
    wproj_t_ref,
    wup_ref,
    wup_t_ref,
    wdown_ref,
    wdown_t_ref,
    spread_ref,
    regroup_ref,
    entry_ref,
    out_left_ref,
    out_own_ref,
    out_right_ref,
    wsum_ref,
    tsum_ref,
    x_s,
    c_s,
    ro_s,
    rg_s,
    qm_s,
    gm_s,
    acc_s,
    accd_s,
    ts_s,
    tt_s,
):
    n_left, n_own, n_right = LEFT * LAT, WW * LAT, RIGHT * LAT

    def place(axis):
        shape = (CELL_ROWS, 1) if axis == 0 else (1, CELL_ROWS)
        cell = lax.broadcasted_iota(jnp.int32, shape, axis)
        col = (cell * 43) >> 8
        base = col * LAT + (cell - col * WH)
        return jnp.concatenate([base + at_ref[s] for s in range(SLOTS)], axis=axis)

    goal = place(0)

    def pick(first, count):
        lane = lax.broadcasted_iota(jnp.int32, (288, count), 1)
        return one_hot(goal - first == lane)

    sel_l = pick(0, n_left)
    sel_o = pick(n_left, n_own)
    sel_r = pick(n_left + n_own, n_right)
    for which, own_ref, scratch in ((0, own_t_ref, x_s), (1, own_c_ref, c_s)):
        got = mm(sel_l, left_ref[which]) + mm(sel_o, own_ref[...]) + mm(sel_r, right_ref[which])
        for slot in range(SLOTS):
            for level in range(LEVELS):
                scratch[slot, level * 72 : level * 72 + 72, :] = got[
                    slot * 72 : slot * 72 + 72, level * WIDTH : (level + 1) * WIDTH
                ].astype(scratch.dtype)

    acc_s[...] = jnp.zeros_like(acc_s)
    accd_s[...] = jnp.zeros_like(accd_s)
    qm_s[...] = jnp.zeros_like(qm_s)
    gm_s[...] = jnp.zeros_like(gm_s)
    tt_s[...] = jnp.zeros_like(tt_s)
    eye_d = eye(WIDTH)
    eye_t = eye(WTOK)
    scale = HEAD ** (-0.5)

    def one_slot(slot, carry):
        x = mm(eye_d, x_s[slot].astype(bf16), NT)
        cot = mm(eye_d, c_s[slot].astype(bf16), NT)
        cot_b = cot.astype(bf16)
        na, inv_a = layer_norm(x)
        na_b = na.astype(bf16)
        qkv = mm(wqkv_t_ref[...], na_b)
        q = (qkv[:WIDTH] * scale).astype(bf16)
        k = qkv[WIDTH : 2 * WIDTH].astype(bf16)
        v = qkv[2 * WIDTH :].astype(bf16)
        k_rows = mm(eye_t, k, NT).astype(bf16)
        v_rows = mm(eye_t, v, NT).astype(bf16)
        for h in range(HEADS):
            qm_s[h * HEAD : (h + 1) * HEAD, h * WTOK : (h + 1) * WTOK] = q[
                h * HEAD : (h + 1) * HEAD
            ]
        qm = qm_s[...]
        scores = mm(k_rows, qm) + bias_ref[slot]
        top = jnp.max(scores, axis=0, keepdims=True)
        exps = jnp.exp(scores - top)
        probs = exps * (1.0 / jnp.sum(exps, axis=0, keepdims=True))
        probs_b = probs.astype(bf16)
        att_b = diagonal(mm(v, probs_b)).astype(bf16)
        hidden = x + mm(wproj_t_ref[...], att_b)
        nb, inv_b = layer_norm(hidden)
        nb_b = nb.astype(bf16)
        pre = mm(wup_t_ref[...], nb_b)
        cdf = 0.5 * (1.0 + lax.erf(pre * 0.7071067811865476))
        density = jnp.exp(-0.5 * pre * pre) * 0.3989422804014327
        act_b = (pre * cdf).astype(bf16)
        slope = cdf + pre * density
        out = hidden + mm(wdown_t_ref[...], act_b)
        ro_s[slot] = mm(eye_t, out.astype(bf16), NT)
        gpre_b = (mm(wdown_ref[...], cot_b) * slope).astype(bf16)
        accd_s[...] += mm(act_b, cot_b, NT)
        gh = cot + norm_back(nb, inv_b, mm(wup_ref[...], gpre_b))
        gh_b = gh.astype(bf16)
        acc_s[:, 768:1536] += mm(nb_b, gpre_b, NT)
        acc_s[:, 576:768] += mm(att_b, gh_b, NT)
        ga = mm(wproj_ref[...], gh_b).astype(bf16)
        for h in range(HEADS):
            gm_s[h * HEAD : (h + 1) * HEAD, h * WTOK : (h + 1) * WTOK] = ga[
                h * HEAD : (h + 1) * HEAD
            ]
        gm = gm_s[...]
        gp = mm(v_rows, gm)
        gs = probs * (gp - jnp.sum(probs * gp, axis=0, keepdims=True))
        gs_b = gs.astype(bf16)
        gq = diagonal(mm(k, gs_b)) * scale
        gk = mm(qm, gs_b, NT)
        gv = mm(gm, probs_b, NT)
        gc_b = jnp.concatenate([gq, gk, gv], axis=0).astype(bf16)
        acc_s[:, 0:576] += mm(na_b, gc_b, NT)
        gt = gh + norm_back(na, inv_a, mm(wqkv_ref[...], gc_b))
        rg_s[slot] = mm(eye_t, gt.astype(bf16), NT)

        heads = [gs[:, h * WTOK : (h + 1) * WTOK] for h in range(HEADS)]
        total = None
        for part in range(PARTS):
            rows = jnp.concatenate(
                [
                    piece[level * 72 + part * 24 : level * 72 + part * 24 + 24]
                    for piece in heads
                    for level in range(LEVELS)
                ],
                axis=0,
            ).astype(bf16)
            term = mm(rows, spread_ref[part], NT)
            total = term if total is None else total + term
        steps = lax.dot_general(
            regroup_ref[...],
            total.astype(bf16),
            (((0,), (0,)), ((), ())),
            preferred_element_type=f32,
        )
        table = steps[216:288]
        for step in range(GROUP - 1):
            table = table + pltpu.roll(steps[step * 72 : step * 72 + 72], GROUP - 1 - step, 1)
        for piece in range(4):
            ts_s[slot, piece * 72 : piece * 72 + 72, 0:69] = table[:, piece * 69 : piece * 69 + 69]
        return carry

    lax.fori_loop(0, SLOTS, one_slot, 0)

    for slot in range(SLOTS):
        values = ts_s[slot][:, 0:69].astype(bf16)
        entries = mm(entry_ref[...], values)
        for n in range(9):
            tt_s[pl.ds(slot * 9 + n, NLON, stride=48), 0:69] = entries[n * NLON : (n + 1) * NLON]
    tsum_ref[...] = tt_s[...].reshape(NLON, 48, 128).astype(bf16)

    for i in range(NLAT):
        quarter = [
            acc_s[12 * i : 12 * i + 12, g * 384 : (g + 1) * 384] for g in range(4)
        ]
        wsum_ref[i, :, 0:384] = jnp.concatenate(quarter, axis=0).astype(bf16)
        wsum_ref[i, :, 384:576] = accd_s[48 * i : 48 * i + 48, :].astype(bf16)

    goal_t = place(1)

    def put(first, count):
        row = lax.broadcasted_iota(jnp.int32, (count, 288), 0)
        return one_hot(goal_t - first == row)

    sets = (put(0, n_left), put(n_left, n_own), put(n_left + n_own, n_right))
    for which, scratch in ((0, ro_s), (1, rg_s)):
        rows = []
        for slot in range(SLOTS):
            block = scratch[slot]
            rows.append(jnp.concatenate([block[0:72], block[72:144]], axis=1))
        rows = jnp.concatenate(rows, axis=0).astype(bf16)
        for sel, ref in zip(sets, (out_left_ref, out_own_ref, out_right_ref)):
            ref[which] = mm(sel, rows).astype(bf16)


def column_pieces(z):
    top = [z[g * 12 : g * 12 + 12, 0:384] for g in range(4)]
    qkv = jnp.concatenate([top[0], top[1][:, 0:192]], axis=1)
    proj = top[1][:, 192:384]
    up = jnp.concatenate([top[2], top[3]], axis=1)
    down = z[:, 384:576]
    return ((qkv, 18, 12), (proj, 6, 12), (up, 24, 12), (down, 6, 48))


def mid_kernel(w_ref, t_ref, out_ref, buf):
    z = w_ref[0].astype(f32)
    for i in range(1, NLAT):
        z = z + w_ref[i].astype(f32)
    buf[...] = jnp.zeros_like(buf)
    place = 4
    for piece, each, rows in column_pieces(z):
        cols = piece.shape[1]
        piece = piece.astype(bf16).astype(f32)
        lane = lax.broadcasted_iota(jnp.int32, (rows, cols), 1)
        owner = lax.broadcasted_iota(jnp.int32, (NLON, cols), 0)
        col_of = lax.broadcasted_iota(jnp.int32, (NLON, cols), 1)
        mine = one_hot((col_of >= owner * each) & (col_of < (owner + 1) * each))
        part = lane - each * lax.div(lane, each)
        stack = jnp.concatenate(
            [jnp.where(part == c, piece, 0.0) for c in range(each)]
            + ([jnp.zeros((4, cols), f32)] if (each * rows) % 8 else []),
            axis=0,
        ).astype(bf16)
        flat = mm(mine, stack, NT)
        count = flat.shape[1]
        for first in range(0, count, 128):
            width = min(128, count - first)
            buf[pl.ds(place, NLON, stride=16), 0:width] = flat[:, first : first + width]
            place += 1
    out_ref[:, 0:32, :] = t_ref[:, 0:32, :]
    tail = t_ref[:, 32:48, :].astype(f32) + buf[...].reshape(NLON, 16, 128)
    out_ref[:, 32:48, :] = tail.astype(bf16)


def fin_kernel(scale, go_ref, in_ref, qkv_ref, proj_ref, up_ref, down_ref, route_ref):
    total = in_ref[0].astype(f32)
    for i in range(1, NLON):
        total = total + in_ref[i].astype(f32)
    place = 36
    for ref, each, rows in ((qkv_ref, 18, 12), (proj_ref, 6, 12), (up_ref, 24, 12), (down_ref, 6, 48)):
        count = each * rows
        lines = -(-count // 128)
        flat = jnp.concatenate([total[place + n : place + n + 1] for n in range(lines)], axis=1)
        place += lines
        wide = lines * 128
        row = lax.broadcasted_iota(jnp.int32, (rows, wide), 0)
        lane = lax.broadcasted_iota(jnp.int32, (rows, wide), 1)
        mine = lane - rows * lax.div(lane, rows) == row
        at = lax.broadcasted_iota(jnp.int32, (wide, each), 0)
        col = lax.broadcasted_iota(jnp.int32, (wide, each), 1)
        hot = jnp.where((at >= col * rows) & (at < (col + 1) * rows), 1.0, 0.0)
        spread = jnp.where(mine, jnp.broadcast_to(flat, (rows, wide)), 0.0)
        ref[...] = lax.dot_general(
            spread, hot, NN, precision=lax.Precision.HIGHEST, preferred_element_type=f32
        ) * scale
    table = total[0:36].astype(bf16).astype(f32)
    for i in range(NLAT):
        for j in range(2):
            mine = jnp.zeros((9, 128), f32)
            for slot in range(SLOTS):
                hit = jnp.where(go_ref[slot] == 2 * i + j, 1.0, 0.0)
                mine = mine + hit * table[slot * 9 : slot * 9 + 9]
            route_ref[i, j * 16 : j * 16 + 16, :] = jnp.concatenate(
                [mine, jnp.zeros((7, 128), f32)], axis=0
            ).astype(bf16)


def table_kernel(in_ref, out_ref):
    total = in_ref[0].astype(f32)
    for i in range(1, NLAT):
        total = total + in_ref[i].astype(f32)
    for j in range(2):
        out_ref[j : j + 1, :] = jnp.concatenate(
            [total[j * 16 + n : j * 16 + n + 1, 0:69] for n in range(9)], axis=1
        )


def vmem():
    return pl.BlockSpec(memory_space=pltpu.VMEM)


def smem():
    return pl.BlockSpec(memory_space=pltpu.SMEM)


def params(mib):
    return pltpu.CompilerParams(vmem_limit_bytes=mib * 1024 * 1024)


def pack(grid):
    return grid.transpose(2, 1, 0, 3).reshape(WW, LAT, LEVELS * WIDTH)


def unpack(cells):
    return cells.reshape(WW, LAT, LEVELS, WIDTH).transpose(2, 1, 0, 3)


def to_lon(x, by):
    count = lax.axis_size("lon")
    return lax.ppermute(x, "lon", [(i, (i + by) % count) for i in range(count)])


def table_bias(rows, spread, regroup):
    shaped = rows.reshape(SLOTS, HEADS, 2, 2, WH, WH * SPAN).transpose(0, 1, 2, 4, 3, 5)
    shaped = shaped.reshape(SLOTS, 72, 2 * WH * SPAN)
    return pl.pallas_call(
        bias_kernel,
        out_shape=jax.ShapeDtypeStruct((SLOTS, WTOK, ALL_Q), f32),
        in_specs=[vmem()] * 3,
        out_specs=vmem(),
        compiler_params=params(40),
        cost_estimate=pl.CostEstimate(flops=1000000000, bytes_accessed=6000000, transcendentals=0),
        name="table_bias",
    )(shaped, spread, regroup)


def block_pass(at, left, own_t, own_c, right, bias, weights, spread, regroup, entry):
    return pl.pallas_call(
        main_kernel,
        out_shape=(
            jax.ShapeDtypeStruct((2, LEFT * LAT, 2 * WIDTH), bf16),
            jax.ShapeDtypeStruct((2, WW * LAT, 2 * WIDTH), bf16),
            jax.ShapeDtypeStruct((2, RIGHT * LAT, 2 * WIDTH), bf16),
            jax.ShapeDtypeStruct((NLAT, 48, 576), bf16),
            jax.ShapeDtypeStruct((NLON, 48, 128), bf16),
        ),
        in_specs=[smem()] + [vmem()] * 16,
        out_specs=(vmem(),) * 5,
        scratch_shapes=[
            pltpu.VMEM((SLOTS, WTOK, WIDTH), f32),
            pltpu.VMEM((SLOTS, WTOK, WIDTH), f32),
            pltpu.VMEM((SLOTS, WTOK, WIDTH), f32),
            pltpu.VMEM((SLOTS, WTOK, WIDTH), f32),
            pltpu.VMEM((WIDTH, ALL_Q), bf16),
            pltpu.VMEM((WIDTH, ALL_Q), bf16),
            pltpu.VMEM((WIDTH, 1536), f32),
            pltpu.VMEM((HID, WIDTH), f32),
            pltpu.VMEM((SLOTS, 288, 128), f32),
            pltpu.VMEM((NLON * 48, 128), f32),
        ],
        compiler_params=params(56),
        name="block_pass",
    )(at, left, own_t, own_c, right, bias, *weights, spread, regroup, entry)


def local(tokens, cotangent, w_qkv, w_proj, w_up, w_down, bias_table, band_rows, lon_shift):
    latwin = bias_table.shape[0]
    lat_index = lax.axis_index("lat")
    band_ends = jnp.cumsum(band_rows)
    my_count = band_rows[lat_index]
    my_start = band_ends[lat_index] - my_count
    slot_ids = jnp.arange(SLOTS, dtype=jnp.int32)
    live = slot_ids < my_count
    row_ids = jnp.minimum(my_start + slot_ids, latwin - 1)
    shift = jnp.take(lon_shift, row_ids, axis=0)
    first = jnp.where(shift <= RIGHT, shift, shift - WW) + LEFT
    at = jnp.where(live, first * LAT + slot_ids * WH, -100000)
    go = jnp.where(live, row_ids, -1)

    own_t = pack(tokens)
    own_c = pack(cotangent)
    both = jnp.stack([own_t, own_c])
    left = to_lon(both[:, WW - LEFT :], 1).reshape(2, LEFT * LAT, 2 * WIDTH)
    right = to_lon(both[:, :RIGHT], -1).reshape(2, RIGHT * LAT, 2 * WIDTH)

    spread = jnp.asarray(spread_table(), bf16)
    regroup = jnp.asarray(regroup_table(), bf16)
    entry = jnp.asarray(entry_table(), bf16)
    bias = table_bias(jnp.take(bias_table, row_ids, axis=0), spread, regroup)
    weights = (w_qkv, w_qkv.T, w_proj, w_proj.T, w_up, w_up.T, w_down, w_down.T)
    out_left, out_own, out_right, w_sums, t_sums = block_pass(
        at,
        left,
        own_t.reshape(WW * LAT, 2 * WIDTH),
        own_c.reshape(WW * LAT, 2 * WIDTH),
        right,
        bias,
        weights,
        spread,
        regroup,
        entry,
    )

    from_right = to_lon(out_left.reshape(2, LEFT, LAT, 2 * WIDTH), -1)
    from_left = to_lon(out_right.reshape(2, RIGHT, LAT, 2 * WIDTH), 1)
    own = out_own.reshape(2, WW, LAT, 2 * WIDTH)
    cells = jnp.concatenate(
        [own[:, :RIGHT] + from_left, own[:, RIGHT : WW - LEFT], own[:, WW - LEFT :] + from_right],
        axis=1,
    )
    output, grad_tokens = unpack(cells[0]), unpack(cells[1])

    w_got = lax.all_to_all(w_sums, "lat", 0, 0)
    lon_send = pl.pallas_call(
        mid_kernel,
        out_shape=jax.ShapeDtypeStruct((NLON, 48, 128), bf16),
        in_specs=[vmem()] * 2,
        out_specs=vmem(),
        scratch_shapes=[pltpu.VMEM((NLON * 16, 128), f32)],
        compiler_params=params(40),
        name="sum_lat",
    )(w_got, t_sums)
    lon_got = lax.all_to_all(lon_send, "lon", 0, 0)
    scale_grad = float(latwin * WH * LEVELS * WW * NLON) ** (-0.5)
    grad_qkv, grad_proj, grad_up, grad_down, route = pl.pallas_call(
        functools.partial(fin_kernel, scale_grad),
        out_shape=(
            jax.ShapeDtypeStruct((12, 18), f32),
            jax.ShapeDtypeStruct((12, 6), f32),
            jax.ShapeDtypeStruct((12, 24), f32),
            jax.ShapeDtypeStruct((48, 6), f32),
            jax.ShapeDtypeStruct((NLAT, 32, 128), bf16),
        ),
        in_specs=[smem(), vmem()],
        out_specs=(vmem(),) * 5,
        compiler_params=params(40),
        name="sum_lon",
    )(go, lon_got)
    route_got = lax.all_to_all(route, "lat", 0, 0)
    grad_table = pl.pallas_call(
        table_kernel,
        out_shape=jax.ShapeDtypeStruct((2, 621), f32),
        in_specs=[vmem()],
        out_specs=vmem(),
        compiler_params=params(40),
        name="sum_table",
    )(route_got)
    return (output, grad_tokens, grad_qkv, grad_proj, grad_up, grad_down, grad_table)


def solution(mesh):
    grid = P(None, "lat", "lon", None)
    cut = P("lat", "lon")
    return jax.shard_map(
        local,
        mesh=mesh,
        in_specs=(grid, grid, P(), P(), P(), P(), P(), P(), P()),
        out_specs=(grid, grid, cut, cut, cut, cut, cut),
        check_vma=False,
    )
```

```python
import functools

import jax
import jax.numpy as jnp
from jax import lax
from jax.experimental import pallas as pl
from jax.experimental.pallas import tpu as pltpu
from jax.sharding import PartitionSpec as P

HEADS = 6
HEAD = 32
WIDTH = 192
HID = 768
WH = 6
WW = 12
LEVELS = 2
SLOTS = 4
WTOK = 144
CELL_ROWS = 72
POS = 3312
SPAN = 23
LEFT = 5
RIGHT = 6
LAT = 24
NLAT = 16
NLON = 32
ALL_Q = HEADS * WTOK
GROUP = 4
PARTS = WW // GROUP
LANES_V = 512
HALF_V = 256
Z = 16
PER_Z = 40

bf16 = jnp.bfloat16
f32 = jnp.float32
epsilon = 1e-05

NN = (((1,), (0,)), ((), ()))
NT = (((1,), (1,)), ((), ()))


def mm(left, right, dims=NN):
    return lax.dot_general(left, right, dims, preferred_element_type=f32)


def one_hot(condition):
    return jnp.where(condition, 1.0, 0.0).astype(bf16)


def eye(count):
    rows = lax.broadcasted_iota(jnp.int32, (count, count), 0)
    cols = lax.broadcasted_iota(jnp.int32, (count, count), 1)
    return one_hot(rows == cols)


def split(x, size):
    high = (x * ((65536 + size - 1) // size)) >> 16
    return high, x - high * size


def tables_kernel(spread_ref, regroup_ref, regroup_t_ref, entry_ref, rows_ref):
    def line(count, axis):
        shape = (count, 1) if axis == 0 else (1, count)
        return lax.broadcasted_iota(jnp.int32, shape, axis)

    level, cell = split(line(WTOK, 1), 72)
    col, row = split(cell, WH)
    source = level * HALF_V + row * SPAN + col + (WW - GROUP)
    place = lax.broadcasted_iota(jnp.int32, (LANES_V, WTOK), 0)
    for part in range(PARTS):
        spread_ref[part] = one_hot(place == source - GROUP * part)

    lane = lax.broadcasted_iota(jnp.int32, (288, 288), 1)
    high, low = split(line(288, 0), 24)
    step, row = split(low, WH)
    regroup_ref[...] = one_hot(lane == step * 72 + high * WH + row)
    step, low = split(line(288, 0), 72)
    high, row = split(low, WH)
    regroup_t_ref[...] = one_hot(lane == (high * GROUP + step) * WH + row)

    place, chunk = split(line(288, 0), NLON)
    at = chunk * 9 + place
    high, hk = split(at >> 1, WH)
    source = ((high & 1) * 2 + (at & 1)) * 72 + (high >> 1) * WH + hk
    entry_ref[...] = one_hot(lane == source)

    high, low = split(line(SLOTS * 144, 0), 72)
    pair, hk = split(low, WH)
    source = ((pair * 2 + (high & 1)) * WH + hk) * 8 + (high >> 1)
    rows_ref[...] = one_hot(lax.broadcasted_iota(jnp.int32, (SLOTS * 144, 1152), 1) == source)


def make_tables():
    return pl.pallas_call(
        tables_kernel,
        out_shape=(
            jax.ShapeDtypeStruct((PARTS, LANES_V, WTOK), bf16),
            jax.ShapeDtypeStruct((288, 288), bf16),
            jax.ShapeDtypeStruct((288, 288), bf16),
            jax.ShapeDtypeStruct((288, 288), bf16),
            jax.ShapeDtypeStruct((SLOTS * 144, 1152), bf16),
        ),
        out_specs=(vmem(),) * 5,
        compiler_params=params(16),
        cost_estimate=pl.CostEstimate(flops=6000000000, bytes_accessed=20000000, transcendentals=0),
        name="index_tables",
    )()


def layer_norm(x):
    centre = jnp.sum(x, axis=0, keepdims=True) * (1.0 / WIDTH)
    shifted = x - centre
    var = jnp.sum(shifted * shifted, axis=0, keepdims=True) * (1.0 / WIDTH)
    inv = lax.rsqrt(var + epsilon)
    return shifted * inv, inv


def norm_back(normed, inv, grad):
    mean_grad = jnp.sum(grad, axis=0, keepdims=True) * (1.0 / WIDTH)
    mean_proj = jnp.sum(grad * normed, axis=0, keepdims=True) * (1.0 / WIDTH)
    return inv * (grad - mean_grad - normed * mean_proj)


def transpose_into(source_ref, target_ref):
    count = source_ref.shape[1]
    for first in range(0, count, 256):
        size = min(256, count - first)
        target_ref[first : first + size, :] = mm(
            eye(size), source_ref[:, first : first + size], NT
        ).astype(bf16)


def prep_kernel(
    lat_ref,
    band_ref,
    table_ref,
    rows_ref,
    spread_ref,
    regroup_ref,
    wqkv_ref,
    wproj_ref,
    wup_ref,
    wdown_t_ref,
    bias_ref,
    wqkv_t_ref,
    wproj_t_ref,
    wup_t_ref,
    wdown_ref,
    flat_s,
    line_s,
):
    start, count = my_rows(lat_ref, band_ref)
    slot_of = lax.broadcasted_iota(jnp.int32, (8, 2 * NLAT), 0)
    row_of = lax.broadcasted_iota(jnp.int32, (8, 2 * NLAT), 1)
    flat_s[...] = mm(one_hot((row_of == start + slot_of) & (slot_of < count)), table_ref[...])
    for i in range(144):
        line_s[i * 8 : i * 8 + 8, 0:138] = flat_s[:, 138 * i : 138 * i + 138]
    lines = mm(rows_ref[...], line_s[:, 0:138].astype(bf16))

    transpose_into(wqkv_ref, wqkv_t_ref)
    transpose_into(wproj_ref, wproj_t_ref)
    transpose_into(wup_ref, wup_t_ref)
    transpose_into(wdown_t_ref, wdown_ref)
    regroup = regroup_ref[...]
    blank = jnp.zeros((72, HALF_V - 138), f32)
    for slot in range(SLOTS):
        at = slot * 144
        rows = jnp.concatenate([lines[at : at + 72], blank, lines[at + 72 : at + 144], blank], axis=1)
        shifted = [
            rows if step == GROUP - 1 else pltpu.roll(rows, LANES_V - (GROUP - 1 - step), 1)
            for step in range(GROUP)
        ]
        stack = jnp.concatenate(shifted, axis=0).astype(bf16)
        left = mm(regroup, stack).astype(bf16)
        for part in range(PARTS):
            full = mm(left, spread_ref[part])
            for head in range(HEADS):
                for level in range(LEVELS):
                    at = (head * 2 + level) * 24
                    bias_ref[
                        slot,
                        level * 72 + part * 24 : level * 72 + part * 24 + 24,
                        head * WTOK : (head + 1) * WTOK,
                    ] = full[at : at + 24, :]


def diagonal(full):
    return jnp.concatenate(
        [
            full[h * HEAD : (h + 1) * HEAD, h * WTOK : (h + 1) * WTOK]
            for h in range(HEADS)
        ],
        axis=0,
    )


def pack_kernel(order_ref, tok_ref, cot_ref, to_right_ref, to_left_ref):
    cut = (WW - LEFT) * LAT
    for which, ref in ((0, tok_ref), (1, cot_ref)):
        low, high = ref[0].astype(f32), ref[1].astype(f32)
        both = jnp.concatenate([low[cut:], high[cut:]], axis=1)
        to_right_ref[which] = both.astype(bf16)
        both = jnp.concatenate([low[: RIGHT * LAT], high[: RIGHT * LAT]], axis=1)
        to_left_ref[which] = both.astype(bf16)


def my_rows(lat_ref, band_ref):
    lat = lat_ref[0]
    start = jnp.int32(0)
    for i in range(NLAT):
        start = start + jnp.where(i < lat, band_ref[i], 0)
    return start, band_ref[lat]


def main_kernel(
    lat_ref,
    half_ref,
    band_ref,
    shift_ref,
    left_ref,
    own_t_ref,
    own_c_ref,
    right_ref,
    bias_ref,
    wqkv_ref,
    wqkv_t_ref,
    wproj_ref,
    wproj_t_ref,
    wup_ref,
    wup_t_ref,
    wdown_ref,
    wdown_t_ref,
    spread_ref,
    regroup_ref,
    entry_ref,
    out_left_ref,
    out_own_ref,
    out_right_ref,
    wsum_ref,
    keep_ref,
    give_ref,
    x_s,
    c_s,
    ro_s,
    rg_s,
    qm_s,
    gm_s,
    acc_s,
    accd_s,
    accq_s,
    ts_s,
    tt_s,
):
    n_left, n_own, n_right = LEFT * LAT, WW * LAT, RIGHT * LAT

    start, count = my_rows(lat_ref, band_ref)
    at = []
    for s in range(SLOTS):
        shift = shift_ref[jnp.minimum(start + s, 2 * NLAT - 1)]
        first = jnp.where(shift <= RIGHT, shift, shift - WW) + LEFT
        at.append(jnp.where(s < count, first * LAT + s * WH, -100000))

    def place(axis):
        shape = (CELL_ROWS, 1) if axis == 0 else (1, CELL_ROWS)
        cell = lax.broadcasted_iota(jnp.int32, shape, axis)
        col = (cell * 43) >> 8
        base = col * LAT + (cell - col * WH)
        return jnp.concatenate([base + at[s] for s in range(SLOTS)], axis=axis)

    goal = place(0)

    def pick(first, count):
        lane = lax.broadcasted_iota(jnp.int32, (288, count), 1)
        return one_hot(goal - first == lane)

    sel_l = pick(0, n_left)
    sel_o = pick(n_left, n_own)
    sel_r = pick(n_left + n_own, n_right)
    for which, own_ref, scratch in ((0, own_t_ref, x_s), (1, own_c_ref, c_s)):
        edge = mm(sel_l, left_ref[which]) + mm(sel_r, right_ref[which])
        for level in range(LEVELS):
            got = edge[:, level * WIDTH : (level + 1) * WIDTH] + mm(sel_o, own_ref[level])
            for slot in range(SLOTS):
                scratch[slot, level * 72 : level * 72 + 72, :] = got[slot * 72 : slot * 72 + 72]

    acc_s[...] = jnp.zeros_like(acc_s)
    accd_s[...] = jnp.zeros_like(accd_s)
    qm_s[...] = jnp.zeros_like(qm_s)
    gm_s[...] = jnp.zeros_like(gm_s)
    tt_s[...] = jnp.zeros_like(tt_s)
    eye_d = eye(WIDTH)
    eye_t = eye(WTOK)
    scale = HEAD ** (-0.5)

    def one_slot(slot):
        x = mm(eye_d, x_s[slot].astype(bf16), NT)
        yield
        cot = mm(eye_d, c_s[slot].astype(bf16), NT)
        yield
        cot_b = cot.astype(bf16)
        na, inv_a = layer_norm(x)
        na_b = na.astype(bf16)
        qkv = mm(wqkv_t_ref[...], na_b)
        yield
        q = (qkv[:WIDTH] * scale).astype(bf16)
        k = qkv[WIDTH : 2 * WIDTH].astype(bf16)
        v = qkv[2 * WIDTH :].astype(bf16)
        k_rows = mm(eye_t, k, NT).astype(bf16)
        yield
        v_rows = mm(eye_t, v, NT).astype(bf16)
        yield
        for h in range(HEADS):
            qm_s[slot, h * HEAD : (h + 1) * HEAD, h * WTOK : (h + 1) * WTOK] = q[
                h * HEAD : (h + 1) * HEAD
            ]
        qm = qm_s[slot]
        scores = mm(k_rows, qm) + bias_ref[slot]
        yield
        top = jnp.max(scores, axis=0, keepdims=True)
        exps = jnp.exp(scores - top)
        probs = exps * (1.0 / jnp.sum(exps, axis=0, keepdims=True))
        probs_b = probs.astype(bf16)
        att_b = diagonal(mm(v, probs_b)).astype(bf16)
        yield
        hidden = x + mm(wproj_t_ref[...], att_b)
        yield
        nb, inv_b = layer_norm(hidden)
        nb_b = nb.astype(bf16)
        pre = mm(wup_t_ref[...], nb_b)
        yield
        cdf = 0.5 * (1.0 + lax.erf(pre * 0.7071067811865476))
        density = jnp.exp(-0.5 * pre * pre) * 0.3989422804014327
        act_b = (pre * cdf).astype(bf16)
        slope = cdf + pre * density
        out = hidden + mm(wdown_t_ref[...], act_b)
        yield
        ro_s[slot] = mm(eye_t, out.astype(bf16), NT)
        yield
        gpre_b = (mm(wdown_ref[...], cot_b) * slope).astype(bf16)
        yield
        accd_s[...] += mm(act_b, cot_b, NT)
        yield
        gh = cot + norm_back(nb, inv_b, mm(wup_ref[...], gpre_b))
        yield
        gh_b = gh.astype(bf16)
        acc_s[:, 768:1536] += mm(nb_b, gpre_b, NT)
        yield
        acc_s[:, 576:768] += mm(att_b, gh_b, NT)
        yield
        ga = mm(wproj_ref[...], gh_b).astype(bf16)
        yield
        for h in range(HEADS):
            gm_s[slot, h * HEAD : (h + 1) * HEAD, h * WTOK : (h + 1) * WTOK] = ga[
                h * HEAD : (h + 1) * HEAD
            ]
        gm = gm_s[slot]
        gp = mm(v_rows, gm)
        yield
        gs = probs * (gp - jnp.sum(probs * gp, axis=0, keepdims=True))
        gs_b = gs.astype(bf16)
        gq = diagonal(mm(k, gs_b)) * scale
        yield
        gk = mm(qm, gs_b, NT)
        yield
        gv = mm(gm, probs_b, NT)
        yield
        gc_b = jnp.concatenate([gq, gk, gv], axis=0).astype(bf16)
        acc_s[:, 0:576] += mm(na_b, gc_b, NT)
        yield
        gt = gh + norm_back(na, inv_a, mm(wqkv_ref[...], gc_b))
        yield
        rg_s[slot] = mm(eye_t, gt.astype(bf16), NT)
        yield

        heads = [gs[:, h * WTOK : (h + 1) * WTOK] for h in range(HEADS)]
        total = None
        for part in range(PARTS):
            rows = jnp.concatenate(
                [
                    piece[level * 72 + part * 24 : level * 72 + part * 24 + 24]
                    for piece in heads
                    for level in range(LEVELS)
                ],
                axis=0,
            ).astype(bf16)
            term = mm(rows, spread_ref[part], NT)
            total = term if total is None else total + term
            yield
        steps = mm(regroup_ref[...], total.astype(bf16))
        yield
        table = steps[216:288]
        for step in range(GROUP - 1):
            table = table + pltpu.roll(steps[step * 72 : step * 72 + 72], GROUP - 1 - step, 1)
        for piece, first in enumerate((0, 69, HALF_V, HALF_V + 69)):
            ts_s[slot, piece * 72 : piece * 72 + 72, 0:69] = table[:, first : first + 69]

    for first in range(0, SLOTS, 4):
        runs = [one_slot(slot) for slot in range(first, first + 4)]
        while runs:
            runs = [run for run in runs if next(run, run) is not run]

    for slot in range(SLOTS):
        values = ts_s[slot][:, 0:69].astype(bf16)
        entries = mm(entry_ref[...], values)
        for n in range(9):
            tt_s[pl.ds(slot * 9 + n, NLON, stride=PER_Z), 0:69] = entries[
                n * NLON : (n + 1) * NLON
            ]
    size = Z * PER_Z
    half = half_ref[0]
    mine = tt_s[pl.ds(pl.multiple_of(half * size, 8), size), :]
    keep_ref[...] = mine.reshape(Z, PER_Z, 128).astype(bf16)
    other = tt_s[pl.ds(pl.multiple_of((1 - half) * size, 8), size), :]
    give_ref[...] = other.reshape(Z, PER_Z, 128).astype(bf16)

    for x in range(2):
        accq_s[:, x * 384 : x * 384 + 288] = acc_s[:, x * 288 : x * 288 + 288]
        accq_s[:, x * 384 + 288 : x * 384 + 384] = acc_s[:, 576 + x * 96 : 576 + x * 96 + 96]
    for x in range(2):
        for i in range(NLAT):
            top = accq_s[12 * i : 12 * i + 12, x * 384 : x * 384 + 384]
            low = acc_s[12 * i : 12 * i + 12, 768 + x * 384 : 768 + x * 384 + 384]
            down = [
                accd_s[48 * i + g * 24 : 48 * i + g * 24 + 24, x * 96 : x * 96 + 96]
                for g in range(2)
            ]
            both = jnp.concatenate([top, low], axis=0)
            wsum_ref[x * NLAT + i] = jnp.concatenate([both] + down, axis=1).astype(bf16)

    goal_t = place(1)

    def put(first, count):
        row = lax.broadcasted_iota(jnp.int32, (count, 288), 0)
        return one_hot(goal_t - first == row)

    put_l, put_o, put_r = put(0, n_left), put(n_left, n_own), put(n_left + n_own, n_right)
    for which, scratch in ((0, ro_s), (1, rg_s)):
        levels = [
            jnp.concatenate(
                [scratch[slot, level * 72 : level * 72 + 72] for slot in range(SLOTS)], axis=0
            )
            for level in range(LEVELS)
        ]
        for level in range(LEVELS):
            out_own_ref[which, level] = mm(put_o, levels[level].astype(bf16)).astype(bf16)
        rows = jnp.concatenate(levels, axis=1).astype(bf16)
        out_left_ref[which] = mm(put_l, rows).astype(bf16)
        out_right_ref[which] = mm(put_r, rows).astype(bf16)


def mid_kernel(
    w_ref,
    keep_ref,
    got_ref,
    own_ref,
    from_left_ref,
    from_right_ref,
    out_ref,
    cells_ref,
    grad_ref,
):
    for which, ref in ((0, cells_ref), (1, grad_ref)):
        for level in range(LEVELS):
            lanes = slice(level * WIDTH, (level + 1) * WIDTH)
            own = own_ref[which, level].astype(f32)
            first, last = from_left_ref[which], from_right_ref[which]
            near, far = RIGHT * LAT, (WW - LEFT) * LAT
            ref[level] = jnp.concatenate(
                [
                    own[:near] + first.astype(f32)[:, lanes],
                    own[near:far],
                    own[far:] + last.astype(f32)[:, lanes],
                ],
                axis=0,
            ).astype(bf16)
    total = w_ref[0].astype(f32)
    for i in range(1, 2 * NLAT):
        total = total + w_ref[i].astype(f32)
    qkv, proj = total[0:12, 0:288], total[0:12, 288:384]
    up = total[12:24, 0:384]
    down = [
        total[0:12, 384:480],
        total[12:24, 384:480],
        total[0:12, 480:576],
        total[12:24, 480:576],
    ]
    for z in range(Z):
        part = jnp.concatenate(
            [
                jnp.concatenate(
                    [qkv[:, 18 * z : 18 * z + 18], proj[:, 6 * z : 6 * z + 6]], axis=1
                ),
                up[:, 24 * z : 24 * z + 24],
                jnp.concatenate([piece[:, 6 * z : 6 * z + 6] for piece in down], axis=1),
                jnp.zeros((PER_Z - 36, 24), f32),
            ],
            axis=0,
        )
        table = keep_ref[z, :, 0:69].astype(f32) + got_ref[z, :, 0:69].astype(f32)
        out_ref[z] = jnp.concatenate(
            [table, part, jnp.zeros((PER_Z, 128 - 93), f32)], axis=1
        ).astype(bf16)


def fin_kernel(scale, lat_ref, band_ref, in_ref, qkv_ref, proj_ref, up_ref, down_ref, route_ref):
    total = in_ref[0].astype(f32)
    for i in range(1, Z):
        total = total + in_ref[i].astype(f32)
    qkv_ref[...] = total[0:12, 69:87] * scale
    proj_ref[...] = total[0:12, 87:93] * scale
    up_ref[...] = total[12:24, 69:93] * scale
    down_ref[...] = (
        jnp.concatenate([total[24:36, 69 + 6 * g : 75 + 6 * g] for g in range(4)], axis=0) * scale
    )
    table = total[0:36].astype(bf16).astype(f32)
    start, count = my_rows(lat_ref, band_ref)
    goes = [jnp.where(slot < count, start + slot, -1) for slot in range(SLOTS)]
    for i in range(NLAT):
        for j in range(2):
            mine = jnp.zeros((9, 128), f32)
            for slot in range(SLOTS):
                hit = jnp.where(goes[slot] == 2 * i + j, 1.0, 0.0)
                mine = mine + hit * table[slot * 9 : slot * 9 + 9]
            route_ref[i, j * 16 : j * 16 + 16, :] = jnp.concatenate(
                [mine, jnp.zeros((7, 128), f32)], axis=0
            ).astype(bf16)


def table_kernel(in_ref, out_ref):
    total = in_ref[0].astype(f32)
    for i in range(1, NLAT):
        total = total + in_ref[i].astype(f32)
    for j in range(2):
        out_ref[j : j + 1, :] = jnp.concatenate(
            [total[j * 16 + n : j * 16 + n + 1, 0:69] for n in range(9)], axis=1
        )


def vmem():
    return pl.BlockSpec(memory_space=pltpu.VMEM)


def smem():
    return pl.BlockSpec(memory_space=pltpu.SMEM)


def params(mib):
    return pltpu.CompilerParams(vmem_limit_bytes=mib * 1024 * 1024)


def to_lon(x, by):
    count = lax.axis_size("lon")
    return lax.ppermute(x, "lon", [(i, (i + by) % count) for i in range(count)])


def prepare(lat, band_rows, bias_table, tables, w_qkv, w_proj, w_up, w_down):
    w_down_t = w_down.T
    bias, w_qkv_t, w_proj_t, w_up_t, w_down = pl.pallas_call(
        prep_kernel,
        out_shape=(
            jax.ShapeDtypeStruct((SLOTS, WTOK, ALL_Q), f32),
            jax.ShapeDtypeStruct((3 * WIDTH, WIDTH), bf16),
            jax.ShapeDtypeStruct((WIDTH, WIDTH), bf16),
            jax.ShapeDtypeStruct((HID, WIDTH), bf16),
            jax.ShapeDtypeStruct((HID, WIDTH), bf16),
        ),
        in_specs=[smem()] * 2 + [vmem()] * 8,
        out_specs=(vmem(),) * 5,
        scratch_shapes=[pltpu.VMEM((8, HEADS * POS), f32), pltpu.VMEM((1152, HALF_V), f32)],
        compiler_params=params(24),
        cost_estimate=pl.CostEstimate(flops=1000000000, bytes_accessed=6000000, transcendentals=0),
        name="prepare",
    )(lat, band_rows, bias_table, *tables, w_qkv, w_proj, w_up, w_down_t)
    return bias, (w_qkv, w_qkv_t, w_proj, w_proj_t, w_up, w_up_t, w_down, w_down_t)


def block_pass(lat, half, band_rows, lon_shift, left, own_t, own_c, right, bias, weights, tables):
    return pl.pallas_call(
        main_kernel,
        out_shape=(
            jax.ShapeDtypeStruct((2, LEFT * LAT, 2 * WIDTH), bf16),
            jax.ShapeDtypeStruct((2, LEVELS, WW * LAT, WIDTH), bf16),
            jax.ShapeDtypeStruct((2, RIGHT * LAT, 2 * WIDTH), bf16),
            jax.ShapeDtypeStruct((2 * NLAT, 24, 576), bf16),
            jax.ShapeDtypeStruct((Z, PER_Z, 128), bf16),
            jax.ShapeDtypeStruct((Z, PER_Z, 128), bf16),
        ),
        in_specs=[smem()] * 4 + [vmem()] * 16,
        out_specs=(vmem(),) * 6,
        scratch_shapes=[
            pltpu.VMEM((SLOTS, WTOK, WIDTH), f32),
            pltpu.VMEM((SLOTS, WTOK, WIDTH), f32),
            pltpu.VMEM((SLOTS, WTOK, WIDTH), f32),
            pltpu.VMEM((SLOTS, WTOK, WIDTH), f32),
            pltpu.VMEM((SLOTS, WIDTH, ALL_Q), bf16),
            pltpu.VMEM((SLOTS, WIDTH, ALL_Q), bf16),
            pltpu.VMEM((WIDTH, 1536), f32),
            pltpu.VMEM((HID, WIDTH), f32),
            pltpu.VMEM((WIDTH, 768), f32),
            pltpu.VMEM((SLOTS, 288, 128), f32),
            pltpu.VMEM((NLON * PER_Z, 128), f32),
        ],
        compiler_params=params(32),
        name="block_pass",
    )(lat, half, band_rows, lon_shift, left, own_t, own_c, right, bias, *weights, *tables)


def local(tokens, cotangent, w_qkv, w_proj, w_up, w_down, bias_table, band_rows, lon_shift):
    latwin = bias_table.shape[0]
    lat = lax.axis_index("lat").reshape(1)
    half = (lax.axis_index("lon") // Z).reshape(1)

    own_t = tokens.transpose(0, 2, 1, 3).reshape(LEVELS, WW * LAT, WIDTH)
    own_c = cotangent.transpose(0, 2, 1, 3).reshape(LEVELS, WW * LAT, WIDTH)
    spread, regroup, regroup_t, entry, rows = make_tables()
    to_right, to_left = pl.pallas_call(
        pack_kernel,
        out_shape=(
            jax.ShapeDtypeStruct((2, LEFT * LAT, 2 * WIDTH), bf16),
            jax.ShapeDtypeStruct((2, RIGHT * LAT, 2 * WIDTH), bf16),
        ),
        in_specs=[pl.BlockSpec(memory_space=pl.ANY)] + [vmem()] * 2,
        out_specs=(vmem(),) * 2,
        compiler_params=params(16),
        name="pack_edges",
    )(regroup, own_t, own_c)
    left = to_lon(to_right, 1)
    right = to_lon(to_left, -1)

    bias, weights = prepare(
        lat, band_rows, bias_table, (rows, spread, regroup), w_qkv, w_proj, w_up, w_down
    )
    out_left, out_own, out_right, w_sums, t_keep, t_give = block_pass(
        lat,
        half,
        band_rows,
        lon_shift,
        left,
        own_t,
        own_c,
        right,
        bias,
        weights,
        (spread, regroup_t, entry),
    )

    from_right = to_lon(out_left, -1)
    from_left = to_lon(out_right, 1)
    t_got = to_lon(t_give, Z)
    near = [[(x * Z + z) * NLAT + i for x in range(2) for i in range(NLAT)] for z in range(Z)]
    ring = [[x * Z + z for z in range(Z)] for x in range(2)]
    w_got = lax.all_to_all(w_sums, ("lon", "lat"), 0, 0, axis_index_groups=near)
    cells_shape = jax.ShapeDtypeStruct((LEVELS, WW * LAT, WIDTH), bf16)
    lon_send, cells, grads = pl.pallas_call(
        mid_kernel,
        out_shape=(jax.ShapeDtypeStruct((Z, PER_Z, 128), bf16), cells_shape, cells_shape),
        in_specs=[vmem()] * 6,
        out_specs=(vmem(),) * 3,
        compiler_params=params(24),
        name="sum_lat",
    )(w_got, t_keep, t_got, out_own, from_left, from_right)
    output = cells.reshape(LEVELS, WW, LAT, WIDTH).transpose(0, 2, 1, 3)
    grad_tokens = grads.reshape(LEVELS, WW, LAT, WIDTH).transpose(0, 2, 1, 3)

    lon_got = lax.all_to_all(lon_send, "lon", 0, 0, axis_index_groups=ring)
    scale_grad = float(latwin * WH * LEVELS * WW * NLON) ** (-0.5)
    grad_qkv, grad_proj, grad_up, grad_down, route = pl.pallas_call(
        functools.partial(fin_kernel, scale_grad),
        out_shape=(
            jax.ShapeDtypeStruct((12, 18), f32),
            jax.ShapeDtypeStruct((12, 6), f32),
            jax.ShapeDtypeStruct((12, 24), f32),
            jax.ShapeDtypeStruct((48, 6), f32),
            jax.ShapeDtypeStruct((NLAT, 32, 128), bf16),
        ),
        in_specs=[smem(), smem(), vmem()],
        out_specs=(vmem(),) * 5,
        compiler_params=params(24),
        name="sum_lon",
    )(lat, band_rows, lon_got)
    route_got = lax.all_to_all(route, "lat", 0, 0)
    grad_table = pl.pallas_call(
        table_kernel,
        out_shape=jax.ShapeDtypeStruct((2, 621), f32),
        in_specs=[vmem()],
        out_specs=vmem(),
        compiler_params=params(24),
        name="sum_table",
    )(route_got)
    return (output, grad_tokens, grad_qkv, grad_proj, grad_up, grad_down, grad_table)


def solution(mesh):
    grid = P(None, "lat", "lon", None)
    cut = P("lat", "lon")
    return jax.shard_map(
        local,
        mesh=mesh,
        in_specs=(grid, grid, P(), P(), P(), P(), P(), P(), P()),
        out_specs=(grid, grid, cut, cut, cut, cut, cut),
        check_vma=False,
    )
```

```python
import functools

import jax
import jax.numpy as jnp
from jax import lax
from jax.experimental import pallas as pl
from jax.experimental.pallas import tpu as pltpu
from jax.sharding import PartitionSpec as P

HEADS = 6
HEAD = 32
WIDTH = 192
HID = 768
WH = 6
WW = 12
LEVELS = 2
SLOTS = 4
WTOK = 144
CELL_ROWS = 72
POS = 3312
SPAN = 23
LEFT = 5
RIGHT = 6
LAT = 24
NLAT = 16
NLON = 32
ALL_Q = HEADS * WTOK
GROUP = 4
PARTS = WW // GROUP
LANES_V = 512
HALF_V = 256
Z = 16
PER_Z = 40
SEND = 32

bf16 = jnp.bfloat16
f32 = jnp.float32
epsilon = 1e-05

NN = (((1,), (0,)), ((), ()))
NT = (((1,), (1,)), ((), ()))


def mm(left, right, dims=NN):
    return lax.dot_general(left, right, dims, preferred_element_type=f32)


def one_hot(condition):
    return jnp.where(condition, 1.0, 0.0).astype(bf16)


def eye(count):
    rows = lax.broadcasted_iota(jnp.int32, (count, count), 0)
    cols = lax.broadcasted_iota(jnp.int32, (count, count), 1)
    return one_hot(rows == cols)


def split(x, size):
    high = (x * ((65536 + size - 1) // size)) >> 16
    return high, x - high * size


def line(count, axis):
    shape = (count, 1) if axis == 0 else (1, count)
    return lax.broadcasted_iota(jnp.int32, shape, axis)


def regroup_matrix():
    high, low = split(line(288, 0), 24)
    step, row = split(low, WH)
    lane = lax.broadcasted_iota(jnp.int32, (288, 288), 1)
    return one_hot(lane == step * 72 + high * WH + row)


def regroup_back_matrix():
    step, low = split(line(288, 0), 72)
    high, row = split(low, WH)
    lane = lax.broadcasted_iota(jnp.int32, (288, 288), 1)
    return one_hot(lane == (high * GROUP + step) * WH + row)


def entry_matrix():
    place, chunk = split(line(288, 0), NLON)
    at = chunk * 9 + place
    high, hk = split(at >> 1, WH)
    source = ((high & 1) * 2 + (at & 1)) * 72 + (high >> 1) * WH + hk
    lane = lax.broadcasted_iota(jnp.int32, (288, 288), 1)
    return one_hot(lane == source)


def tables_kernel(spread_ref, rows_ref):
    level, cell = split(line(WTOK, 1), 72)
    col, row = split(cell, WH)
    source = level * HALF_V + row * SPAN + col + (WW - GROUP)
    place = lax.broadcasted_iota(jnp.int32, (LANES_V, WTOK), 0)
    for part in range(PARTS):
        spread_ref[part] = one_hot(place == source - GROUP * part)

    high, low = split(line(SLOTS * 144, 0), 72)
    pair, hk = split(low, WH)
    source = ((pair * 2 + (high & 1)) * WH + hk) * 8 + (high >> 1)
    rows_ref[...] = one_hot(lax.broadcasted_iota(jnp.int32, (SLOTS * 144, 1152), 1) == source)


def make_tables():
    return pl.pallas_call(
        tables_kernel,
        out_shape=(
            jax.ShapeDtypeStruct((PARTS, LANES_V, WTOK), bf16),
            jax.ShapeDtypeStruct((SLOTS * 144, 1152), bf16),
        ),
        out_specs=(vmem(),) * 2,
        compiler_params=params(16),
        cost_estimate=pl.CostEstimate(flops=6000000000, bytes_accessed=20000000, transcendentals=0),
        name="index_tables",
    )()


def layer_norm(x):
    centre = jnp.sum(x, axis=0, keepdims=True) * (1.0 / WIDTH)
    shifted = x - centre
    var = jnp.sum(shifted * shifted, axis=0, keepdims=True) * (1.0 / WIDTH)
    inv = lax.rsqrt(var + epsilon)
    return shifted * inv, inv


def norm_back(normed, inv, grad):
    mean_grad = jnp.sum(grad, axis=0, keepdims=True) * (1.0 / WIDTH)
    mean_proj = jnp.sum(grad * normed, axis=0, keepdims=True) * (1.0 / WIDTH)
    return inv * (grad - mean_grad - normed * mean_proj)


def transpose_into(source_ref, target_ref):
    count = source_ref.shape[1]
    for first in range(0, count, 256):
        size = min(256, count - first)
        target_ref[first : first + size, :] = mm(
            eye(size), source_ref[:, first : first + size], NT
        ).astype(bf16)


def prep_kernel(
    lat_ref,
    band_ref,
    table_ref,
    rows_ref,
    spread_ref,
    bias_ref,
    flat_s,
    line_s,
):
    start, count = my_rows(lat_ref, band_ref)
    slot_of = lax.broadcasted_iota(jnp.int32, (8, 2 * NLAT), 0)
    row_of = lax.broadcasted_iota(jnp.int32, (8, 2 * NLAT), 1)
    flat_s[...] = mm(one_hot((row_of == start + slot_of) & (slot_of < count)), table_ref[...])
    for i in range(144):
        line_s[i * 8 : i * 8 + 8, 0:138] = flat_s[:, 138 * i : 138 * i + 138]
    lines = mm(rows_ref[...], line_s[:, 0:138].astype(bf16))

    regroup = regroup_matrix()
    blank = jnp.zeros((72, HALF_V - 138), f32)
    for slot in range(SLOTS):
        at = slot * 144
        rows = jnp.concatenate([lines[at : at + 72], blank, lines[at + 72 : at + 144], blank], axis=1)
        shifted = [
            rows if step == GROUP - 1 else pltpu.roll(rows, LANES_V - (GROUP - 1 - step), 1)
            for step in range(GROUP)
        ]
        stack = jnp.concatenate(shifted, axis=0).astype(bf16)
        left = mm(regroup, stack).astype(bf16)
        for part in range(PARTS):
            full = mm(left, spread_ref[part])
            for head in range(HEADS):
                for level in range(LEVELS):
                    at = (head * 2 + level) * 24
                    bias_ref[
                        slot,
                        level * 72 + part * 24 : level * 72 + part * 24 + 24,
                        head * WTOK : (head + 1) * WTOK,
                    ] = full[at : at + 24, :]


def diagonal(full):
    return jnp.concatenate(
        [
            full[h * HEAD : (h + 1) * HEAD, h * WTOK : (h + 1) * WTOK]
            for h in range(HEADS)
        ],
        axis=0,
    )


def pack_kernel(order_ref, tok_ref, cot_ref, to_right_ref, to_left_ref):
    cut = (WW - LEFT) * LAT
    for which, ref in ((0, tok_ref), (1, cot_ref)):
        low, high = ref[0].astype(f32), ref[1].astype(f32)
        both = jnp.concatenate([low[cut:], high[cut:]], axis=1)
        to_right_ref[which] = both.astype(bf16)
        both = jnp.concatenate([low[: RIGHT * LAT], high[: RIGHT * LAT]], axis=1)
        to_left_ref[which] = both.astype(bf16)


def my_rows(lat_ref, band_ref):
    lat = lat_ref[0]
    start = jnp.int32(0)
    for i in range(NLAT):
        start = start + jnp.where(i < lat, band_ref[i], 0)
    return start, band_ref[lat]


def early_kernel(
    lat_ref,
    band_ref,
    shift_ref,
    own_t_ref,
    own_c_ref,
    wqkv_ref,
    wproj_ref,
    wup_ref,
    wdown_t_ref,
    x_own_ref,
    c_own_ref,
    sel_l_ref,
    sel_r_ref,
    put_l_ref,
    put_o_ref,
    put_r_ref,
    wqkv_t_ref,
    wproj_t_ref,
    wup_t_ref,
    wdown_ref,
    regroup_ref,
    entry_ref,
):
    regroup_ref[...] = regroup_back_matrix()
    entry_ref[...] = entry_matrix()
    n_left, n_own, n_right = LEFT * LAT, WW * LAT, RIGHT * LAT

    start, count = my_rows(lat_ref, band_ref)
    at = []
    for s in range(SLOTS):
        shift = shift_ref[jnp.minimum(start + s, 2 * NLAT - 1)]
        first = jnp.where(shift <= RIGHT, shift, shift - WW) + LEFT
        at.append(jnp.where(s < count, first * LAT + s * WH, -100000))

    def place(axis):
        shape = (CELL_ROWS, 1) if axis == 0 else (1, CELL_ROWS)
        cell = lax.broadcasted_iota(jnp.int32, shape, axis)
        col = (cell * 43) >> 8
        base = col * LAT + (cell - col * WH)
        return jnp.concatenate([base + at[s] for s in range(SLOTS)], axis=axis)

    goal = place(0)

    def pick(first, count):
        lane = lax.broadcasted_iota(jnp.int32, (288, count), 1)
        return one_hot(goal - first == lane)

    sel_l_ref[...] = pick(0, n_left)
    sel_r_ref[...] = pick(n_left + n_own, n_right)
    sel_o = pick(n_left, n_own)
    for own_ref, into_ref in ((own_t_ref, x_own_ref), (own_c_ref, c_own_ref)):
        for level in range(LEVELS):
            got = mm(sel_o, own_ref[level])
            for slot in range(SLOTS):
                into_ref[slot, level * 72 : level * 72 + 72, :] = got[slot * 72 : slot * 72 + 72]

    goal_t = place(1)

    def put(first, count):
        row = lax.broadcasted_iota(jnp.int32, (count, 288), 0)
        return one_hot(goal_t - first == row)

    put_l_ref[...] = put(0, n_left)
    put_o_ref[...] = put(n_left, n_own)
    put_r_ref[...] = put(n_left + n_own, n_right)

    transpose_into(wqkv_ref, wqkv_t_ref)
    transpose_into(wproj_ref, wproj_t_ref)
    transpose_into(wup_ref, wup_t_ref)
    transpose_into(wdown_t_ref, wdown_ref)


def main_kernel(
    half_ref,
    left_ref,
    right_ref,
    x_own_ref,
    c_own_ref,
    sel_l_ref,
    sel_r_ref,
    put_l_ref,
    put_o_ref,
    put_r_ref,
    bias_ref,
    wqkv_ref,
    wqkv_t_ref,
    wproj_ref,
    wproj_t_ref,
    wup_ref,
    wup_t_ref,
    wdown_ref,
    wdown_t_ref,
    spread_ref,
    regroup_ref,
    entry_ref,
    out_left_ref,
    out_own_ref,
    out_right_ref,
    wsum_ref,
    keep_ref,
    give_ref,
    x_s,
    c_s,
    ro_s,
    rg_s,
    qm_s,
    gm_s,
    acc_s,
    accd_s,
    accq_s,
    ts_s,
    tt_s,
):
    for which, own_ref, scratch in ((0, x_own_ref, x_s), (1, c_own_ref, c_s)):
        edge = mm(sel_l_ref[...], left_ref[which]) + mm(sel_r_ref[...], right_ref[which])
        for level in range(LEVELS):
            for slot in range(SLOTS):
                rows = slice(level * 72, level * 72 + 72)
                scratch[slot, rows, :] = (
                    own_ref[slot, rows, :]
                    + edge[slot * 72 : slot * 72 + 72, level * WIDTH : (level + 1) * WIDTH]
                )

    acc_s[...] = jnp.zeros_like(acc_s)
    accd_s[...] = jnp.zeros_like(accd_s)
    qm_s[...] = jnp.zeros_like(qm_s)
    gm_s[...] = jnp.zeros_like(gm_s)
    tt_s[...] = jnp.zeros_like(tt_s)
    eye_d = eye(WIDTH)
    eye_t = eye(WTOK)
    scale = HEAD ** (-0.5)

    def one_slot(slot):
        x = mm(eye_d, x_s[slot].astype(bf16), NT)
        yield
        cot = mm(eye_d, c_s[slot].astype(bf16), NT)
        yield
        cot_b = cot.astype(bf16)
        na, inv_a = layer_norm(x)
        na_b = na.astype(bf16)
        qkv = mm(wqkv_t_ref[...], na_b)
        yield
        q = (qkv[:WIDTH] * scale).astype(bf16)
        k = qkv[WIDTH : 2 * WIDTH].astype(bf16)
        v = qkv[2 * WIDTH :].astype(bf16)
        k_rows = mm(eye_t, k, NT).astype(bf16)
        yield
        v_rows = mm(eye_t, v, NT).astype(bf16)
        yield
        for h in range(HEADS):
            qm_s[slot, h * HEAD : (h + 1) * HEAD, h * WTOK : (h + 1) * WTOK] = q[
                h * HEAD : (h + 1) * HEAD
            ]
        qm = qm_s[slot]
        scores = mm(k_rows, qm) + bias_ref[slot]
        yield
        top = jnp.max(scores, axis=0, keepdims=True)
        exps = jnp.exp(scores - top)
        probs = exps * (1.0 / jnp.sum(exps, axis=0, keepdims=True))
        probs_b = probs.astype(bf16)
        att_b = diagonal(mm(v, probs_b)).astype(bf16)
        yield
        hidden = x + mm(wproj_t_ref[...], att_b)
        yield
        nb, inv_b = layer_norm(hidden)
        nb_b = nb.astype(bf16)
        pre = mm(wup_t_ref[...], nb_b)
        yield
        cdf = 0.5 * (1.0 + lax.erf(pre * 0.7071067811865476))
        density = jnp.exp(-0.5 * pre * pre) * 0.3989422804014327
        act_b = (pre * cdf).astype(bf16)
        slope = cdf + pre * density
        out = hidden + mm(wdown_t_ref[...], act_b)
        yield
        ro_s[slot] = mm(eye_t, out.astype(bf16), NT)
        yield
        gpre_b = (mm(wdown_ref[...], cot_b) * slope).astype(bf16)
        yield
        accd_s[...] += mm(act_b, cot_b, NT)
        yield
        gh = cot + norm_back(nb, inv_b, mm(wup_ref[...], gpre_b))
        yield
        gh_b = gh.astype(bf16)
        acc_s[:, 768:1536] += mm(nb_b, gpre_b, NT)
        yield
        acc_s[:, 576:768] += mm(att_b, gh_b, NT)
        yield
        ga = mm(wproj_ref[...], gh_b).astype(bf16)
        yield
        for h in range(HEADS):
            gm_s[slot, h * HEAD : (h + 1) * HEAD, h * WTOK : (h + 1) * WTOK] = ga[
                h * HEAD : (h + 1) * HEAD
            ]
        gm = gm_s[slot]
        gp = mm(v_rows, gm)
        yield
        gs = probs * (gp - jnp.sum(probs * gp, axis=0, keepdims=True))
        gs_b = gs.astype(bf16)
        gq = diagonal(mm(k, gs_b)) * scale
        yield
        gk = mm(qm, gs_b, NT)
        yield
        gv = mm(gm, probs_b, NT)
        yield
        gc_b = jnp.concatenate([gq, gk, gv], axis=0).astype(bf16)
        acc_s[:, 0:576] += mm(na_b, gc_b, NT)
        yield
        gt = gh + norm_back(na, inv_a, mm(wqkv_ref[...], gc_b))
        yield
        rg_s[slot] = mm(eye_t, gt.astype(bf16), NT)
        yield

        heads = [gs[:, h * WTOK : (h + 1) * WTOK] for h in range(HEADS)]
        total = None
        for part in range(PARTS):
            rows = jnp.concatenate(
                [
                    piece[level * 72 + part * 24 : level * 72 + part * 24 + 24]
                    for piece in heads
                    for level in range(LEVELS)
                ],
                axis=0,
            ).astype(bf16)
            term = mm(rows, spread_ref[part], NT)
            total = term if total is None else total + term
            yield
        steps = mm(regroup_ref[...], total.astype(bf16))
        yield
        table = steps[216:288]
        for step in range(GROUP - 1):
            table = table + pltpu.roll(steps[step * 72 : step * 72 + 72], GROUP - 1 - step, 1)
        for piece, first in enumerate((0, 69, HALF_V, HALF_V + 69)):
            ts_s[slot, piece * 72 : piece * 72 + 72, 0:69] = table[:, first : first + 69]

    for first in range(0, SLOTS, 4):
        runs = [one_slot(slot) for slot in range(first, first + 4)]
        while runs:
            runs = [run for run in runs if next(run, run) is not run]

    for slot in range(SLOTS):
        values = ts_s[slot][:, 0:69].astype(bf16)
        entries = mm(entry_ref[...], values)
        for n in range(9):
            tt_s[pl.ds(slot * 9 + n, NLON, stride=PER_Z), 0:69] = entries[
                n * NLON : (n + 1) * NLON
            ]
    size = Z * PER_Z
    half = half_ref[0]
    mine = tt_s[pl.ds(pl.multiple_of(half * size, 8), size), :]
    keep_ref[...] = mine.reshape(Z, PER_Z, 128).astype(bf16)
    other = tt_s[pl.ds(pl.multiple_of((1 - half) * size, 8), size), :]
    give_ref[...] = other.reshape(Z, PER_Z, 128).astype(bf16)

    for x in range(2):
        accq_s[:, x * 384 : x * 384 + 288] = acc_s[:, x * 288 : x * 288 + 288]
        accq_s[:, x * 384 + 288 : x * 384 + 384] = acc_s[:, 576 + x * 96 : 576 + x * 96 + 96]
    for x in range(2):
        for i in range(NLAT):
            top = accq_s[12 * i : 12 * i + 12, x * 384 : x * 384 + 384]
            low = acc_s[12 * i : 12 * i + 12, 768 + x * 384 : 768 + x * 384 + 384]
            down = [
                accd_s[48 * i + g * 24 : 48 * i + g * 24 + 24, x * 96 : x * 96 + 96]
                for g in range(2)
            ]
            both = jnp.concatenate([top, low], axis=0)
            wsum_ref[x * NLAT + i] = jnp.concatenate([both] + down, axis=1).astype(bf16)

    for which, scratch in ((0, ro_s), (1, rg_s)):
        levels = [
            jnp.concatenate(
                [scratch[slot, level * 72 : level * 72 + 72] for slot in range(SLOTS)], axis=0
            )
            for level in range(LEVELS)
        ]
        for level in range(LEVELS):
            out_own_ref[which, level] = mm(put_o_ref[...], levels[level].astype(bf16)).astype(bf16)
        rows = jnp.concatenate(levels, axis=1).astype(bf16)
        out_left_ref[which] = mm(put_l_ref[...], rows).astype(bf16)
        out_right_ref[which] = mm(put_r_ref[...], rows).astype(bf16)


def mid_kernel(
    w_ref,
    keep_ref,
    got_ref,
    out_ref,
):
    total = w_ref[0].astype(f32)
    for i in range(1, 2 * NLAT):
        total = total + w_ref[i].astype(f32)
    qkv, proj = total[0:12, 0:288], total[0:12, 288:384]
    up = total[12:24, 0:384]
    down = [
        total[0:12, 384:480],
        total[12:24, 384:480],
        total[0:12, 480:576],
        total[12:24, 480:576],
    ]
    for z in range(Z):
        part = jnp.concatenate(
            [
                jnp.concatenate(
                    [qkv[:, 18 * z : 18 * z + 18], proj[:, 6 * z : 6 * z + 6]], axis=1
                ),
                up[:, 24 * z : 24 * z + 24],
                jnp.concatenate([piece[:, 6 * z : 6 * z + 6] for piece in down], axis=1),
            ],
            axis=0,
        )
        table = keep_ref[z, :, 0:69].astype(f32) + got_ref[z, :, 0:69].astype(f32)
        rest = jnp.concatenate(
            [
                jnp.concatenate([table[32:36, 23 * n : 23 * n + 23] for n in range(3)], axis=0),
                part[32:36, 0:23],
            ],
            axis=0,
        )
        rest = jnp.concatenate([rest, jnp.zeros((SEND - 16, 23), f32)], axis=0)
        last = jnp.concatenate([jnp.zeros((12, 1), f32), part[32:36, 23:24]], axis=0)
        last = jnp.concatenate([last, jnp.zeros((SEND - 16, 1), f32)], axis=0)
        out_ref[z] = jnp.concatenate(
            [table[0:SEND], part[0:SEND], rest, last, jnp.zeros((SEND, 11), f32)], axis=1
        ).astype(bf16)


def cells_kernel(own_ref, from_left_ref, from_right_ref, cells_ref, grad_ref):
    for which, ref in ((0, cells_ref), (1, grad_ref)):
        for level in range(LEVELS):
            lanes = slice(level * WIDTH, (level + 1) * WIDTH)
            own = own_ref[which, level].astype(f32)
            first, last = from_left_ref[which], from_right_ref[which]
            near, far = RIGHT * LAT, (WW - LEFT) * LAT
            ref[level] = jnp.concatenate(
                [
                    own[:near] + first.astype(f32)[:, lanes],
                    own[near:far],
                    own[far:] + last.astype(f32)[:, lanes],
                ],
                axis=0,
            ).astype(bf16)


def fin_kernel(scale, lat_ref, band_ref, in_ref, qkv_ref, proj_ref, up_ref, down_ref, route_ref):
    total = in_ref[0].astype(f32)
    for i in range(1, Z):
        total = total + in_ref[i].astype(f32)
    extra = jnp.concatenate([total[4 * n : 4 * n + 4, 93:116] for n in range(3)], axis=1)
    extra = jnp.concatenate([extra, total[12:16, 93:117], jnp.zeros((4, 35), f32)], axis=1)
    total = jnp.concatenate([total, extra], axis=0)
    qkv_ref[...] = total[0:12, 69:87] * scale
    proj_ref[...] = total[0:12, 87:93] * scale
    up_ref[...] = total[12:24, 69:93] * scale
    down_ref[...] = (
        jnp.concatenate([total[24:36, 69 + 6 * g : 75 + 6 * g] for g in range(4)], axis=0) * scale
    )
    table = total[0:36].astype(bf16).astype(f32)
    start, count = my_rows(lat_ref, band_ref)
    goes = [jnp.where(slot < count, start + slot, -1) for slot in range(SLOTS)]
    for i in range(NLAT):
        for j in range(2):
            mine = jnp.zeros((9, 128), f32)
            for slot in range(SLOTS):
                hit = jnp.where(goes[slot] == 2 * i + j, 1.0, 0.0)
                mine = mine + hit * table[slot * 9 : slot * 9 + 9]
            route_ref[i, j * 16 : j * 16 + 16, :] = jnp.concatenate(
                [mine, jnp.zeros((7, 128), f32)], axis=0
            ).astype(bf16)


def table_kernel(in_ref, out_ref):
    total = in_ref[0].astype(f32)
    for i in range(1, NLAT):
        total = total + in_ref[i].astype(f32)
    for j in range(2):
        out_ref[j : j + 1, :] = jnp.concatenate(
            [total[j * 16 + n : j * 16 + n + 1, 0:69] for n in range(9)], axis=1
        )


def vmem():
    return pl.BlockSpec(memory_space=pltpu.VMEM)


def smem():
    return pl.BlockSpec(memory_space=pltpu.SMEM)


def params(mib):
    return pltpu.CompilerParams(vmem_limit_bytes=mib * 1024 * 1024)


def to_lon(x, by):
    count = lax.axis_size("lon")
    return lax.ppermute(x, "lon", [(i, (i + by) % count) for i in range(count)])


def prepare(lat, band_rows, bias_table, tables):
    return pl.pallas_call(
        prep_kernel,
        out_shape=jax.ShapeDtypeStruct((SLOTS, WTOK, ALL_Q), f32),
        in_specs=[smem()] * 2 + [vmem()] * 3,
        out_specs=vmem(),
        scratch_shapes=[pltpu.VMEM((8, HEADS * POS), f32), pltpu.VMEM((1152, HALF_V), f32)],
        compiler_params=params(24),
        cost_estimate=pl.CostEstimate(flops=1000000000, bytes_accessed=6000000, transcendentals=0),
        name="prepare",
    )(lat, band_rows, bias_table, *tables)


def early_part(lat, band_rows, lon_shift, own_t, own_c, w_qkv, w_proj, w_up, w_down_t):
    windows = jax.ShapeDtypeStruct((SLOTS, WTOK, WIDTH), f32)
    n_left, n_own, n_right = LEFT * LAT, WW * LAT, RIGHT * LAT
    shapes = ((288, n_left), (288, n_right), (n_left, 288), (n_own, 288), (n_right, 288))
    flips = ((3 * WIDTH, WIDTH), (WIDTH, WIDTH), (HID, WIDTH), (HID, WIDTH))
    flips = flips + ((288, 288), (288, 288))
    return pl.pallas_call(
        early_kernel,
        out_shape=(windows, windows)
        + tuple(jax.ShapeDtypeStruct(shape, bf16) for shape in shapes + flips),
        in_specs=[smem()] * 3 + [vmem()] * 6,
        out_specs=(vmem(),) * 13,
        compiler_params=params(24),
        cost_estimate=pl.CostEstimate(flops=1000000000, bytes_accessed=6000000, transcendentals=0),
        name="own_cells",
    )(lat, band_rows, lon_shift, own_t, own_c, w_qkv, w_proj, w_up, w_down_t)


def block_pass(half, left, right, early, bias, weights, tables):
    return pl.pallas_call(
        main_kernel,
        out_shape=(
            jax.ShapeDtypeStruct((2, LEFT * LAT, 2 * WIDTH), bf16),
            jax.ShapeDtypeStruct((2, LEVELS, WW * LAT, WIDTH), bf16),
            jax.ShapeDtypeStruct((2, RIGHT * LAT, 2 * WIDTH), bf16),
            jax.ShapeDtypeStruct((2 * NLAT, 24, 576), bf16),
            jax.ShapeDtypeStruct((Z, PER_Z, 128), bf16),
            jax.ShapeDtypeStruct((Z, PER_Z, 128), bf16),
        ),
        in_specs=[smem()] + [vmem()] * 21,
        out_specs=(vmem(),) * 6,
        scratch_shapes=[
            pltpu.VMEM((SLOTS, WTOK, WIDTH), f32),
            pltpu.VMEM((SLOTS, WTOK, WIDTH), f32),
            pltpu.VMEM((SLOTS, WTOK, WIDTH), f32),
            pltpu.VMEM((SLOTS, WTOK, WIDTH), f32),
            pltpu.VMEM((SLOTS, WIDTH, ALL_Q), bf16),
            pltpu.VMEM((SLOTS, WIDTH, ALL_Q), bf16),
            pltpu.VMEM((WIDTH, 1536), f32),
            pltpu.VMEM((HID, WIDTH), f32),
            pltpu.VMEM((WIDTH, 768), f32),
            pltpu.VMEM((SLOTS, 288, 128), f32),
            pltpu.VMEM((NLON * PER_Z, 128), f32),
        ],
        compiler_params=params(32),
        name="block_pass",
    )(half, left, right, *early, bias, *weights, *tables)


def local(tokens, cotangent, w_qkv, w_proj, w_up, w_down, bias_table, band_rows, lon_shift):
    latwin = bias_table.shape[0]
    lat = lax.axis_index("lat").reshape(1)
    half = (lax.axis_index("lon") // Z).reshape(1)

    own_t = tokens.transpose(0, 2, 1, 3).reshape(LEVELS, WW * LAT, WIDTH)
    own_c = cotangent.transpose(0, 2, 1, 3).reshape(LEVELS, WW * LAT, WIDTH)
    spread, rows = make_tables()
    to_right, to_left = pl.pallas_call(
        pack_kernel,
        out_shape=(
            jax.ShapeDtypeStruct((2, LEFT * LAT, 2 * WIDTH), bf16),
            jax.ShapeDtypeStruct((2, RIGHT * LAT, 2 * WIDTH), bf16),
        ),
        in_specs=[pl.BlockSpec(memory_space=pl.ANY)] + [vmem()] * 2,
        out_specs=(vmem(),) * 2,
        compiler_params=params(16),
        name="pack_edges",
    )(rows, own_t, own_c)
    left = to_lon(to_right, 1)
    right = to_lon(to_left, -1)

    bias = prepare(lat, band_rows, bias_table, (rows, spread))
    w_down_t = w_down.T
    early = early_part(
        lat, band_rows, lon_shift, own_t, own_c, w_qkv, w_proj, w_up, w_down_t
    )
    flip = early[7:]
    weights = (w_qkv, flip[0], w_proj, flip[1], w_up, flip[2], flip[3], w_down_t)
    out_left, out_own, out_right, w_sums, t_keep, t_give = block_pass(
        half, left, right, early[:7], bias, weights, (spread, flip[4], flip[5])
    )

    t_got = to_lon(t_give, Z)
    from_right = to_lon(out_left, -1)
    from_left = to_lon(out_right, 1)
    near = [[(x * Z + z) * NLAT + i for x in range(2) for i in range(NLAT)] for z in range(Z)]
    ring = [[x * Z + z for z in range(Z)] for x in range(2)]
    w_got = lax.all_to_all(w_sums, ("lon", "lat"), 0, 0, axis_index_groups=near)
    cells_shape = jax.ShapeDtypeStruct((LEVELS, WW * LAT, WIDTH), bf16)
    w_got, t_got, from_left, from_right = lax.optimization_barrier(
        (w_got, t_got, from_left, from_right)
    )
    cells, grads = pl.pallas_call(
        cells_kernel,
        out_shape=(cells_shape, cells_shape),
        in_specs=[vmem()] * 3,
        out_specs=(vmem(),) * 2,
        compiler_params=params(16),
        cost_estimate=pl.CostEstimate(flops=100000000, bytes_accessed=3000000, transcendentals=0),
        name="join_cells",
    )(out_own, from_left, from_right)
    lon_send = pl.pallas_call(
        mid_kernel,
        out_shape=jax.ShapeDtypeStruct((Z, SEND, 128), bf16),
        in_specs=[vmem()] * 3,
        out_specs=vmem(),
        compiler_params=params(24),
        name="sum_lat",
    )(w_got, t_keep, t_got)
    output = cells.reshape(LEVELS, WW, LAT, WIDTH).transpose(0, 2, 1, 3)
    grad_tokens = grads.reshape(LEVELS, WW, LAT, WIDTH).transpose(0, 2, 1, 3)

    lon_got = lax.all_to_all(lon_send, "lon", 0, 0, axis_index_groups=ring)
    scale_grad = float(latwin * WH * LEVELS * WW * NLON) ** (-0.5)
    grad_qkv, grad_proj, grad_up, grad_down, route = pl.pallas_call(
        functools.partial(fin_kernel, scale_grad),
        out_shape=(
            jax.ShapeDtypeStruct((12, 18), f32),
            jax.ShapeDtypeStruct((12, 6), f32),
            jax.ShapeDtypeStruct((12, 24), f32),
            jax.ShapeDtypeStruct((48, 6), f32),
            jax.ShapeDtypeStruct((NLAT, 32, 128), bf16),
        ),
        in_specs=[smem(), smem(), vmem()],
        out_specs=(vmem(),) * 5,
        compiler_params=params(24),
        name="sum_lon",
    )(lat, band_rows, lon_got)
    route_got = lax.all_to_all(route, "lat", 0, 0)
    grad_table = pl.pallas_call(
        table_kernel,
        out_shape=jax.ShapeDtypeStruct((2, 621), f32),
        in_specs=[vmem()],
        out_specs=vmem(),
        compiler_params=params(24),
        name="sum_table",
    )(route_got)
    return (output, grad_tokens, grad_qkv, grad_proj, grad_up, grad_down, grad_table)


def solution(mesh):
    grid = P(None, "lat", "lon", None)
    cut = P("lat", "lon")
    return jax.shard_map(
        local,
        mesh=mesh,
        in_specs=(grid, grid, P(), P(), P(), P(), P(), P(), P()),
        out_specs=(grid, grid, cut, cut, cut, cut, cut),
        check_vma=False,
    )
```

```python
import functools

import jax
import jax.numpy as jnp
from jax import lax
from jax.experimental import pallas as pl
from jax.experimental.pallas import tpu as pltpu
from jax.sharding import PartitionSpec as P

HEADS = 6
HEAD = 32
WIDTH = 192
HID = 768
WH = 6
WW = 12
LEVELS = 2
SLOTS = 4
WTOK = 144
CELL_ROWS = 72
POS = 3312
SPAN = 23
LEFT = 5
RIGHT = 6
LAT = 24
NLAT = 16
NLON = 32
ALL_Q = HEADS * WTOK
GROUP = 4
PARTS = WW // GROUP
LANES_V = 512
HALF_V = 256
Z = 16
PER_Z = 40
SEND = 32

bf16 = jnp.bfloat16
f32 = jnp.float32
epsilon = 1e-05

NN = (((1,), (0,)), ((), ()))
NT = (((1,), (1,)), ((), ()))


def mm(left, right, dims=NN):
    return lax.dot_general(left, right, dims, preferred_element_type=f32)


def one_hot(condition):
    return jnp.where(condition, 1.0, 0.0).astype(bf16)


def eye(count):
    rows = lax.broadcasted_iota(jnp.int32, (count, count), 0)
    cols = lax.broadcasted_iota(jnp.int32, (count, count), 1)
    return one_hot(rows == cols)


def split(x, size):
    high = (x * ((65536 + size - 1) // size)) >> 16
    return high, x - high * size


def line(count, axis):
    shape = (count, 1) if axis == 0 else (1, count)
    return lax.broadcasted_iota(jnp.int32, shape, axis)


def regroup_matrix():
    high, low = split(line(288, 0), 24)
    step, row = split(low, WH)
    lane = lax.broadcasted_iota(jnp.int32, (288, 288), 1)
    return one_hot(lane == step * 72 + high * WH + row)


def regroup_back_matrix():
    step, low = split(line(288, 0), 72)
    high, row = split(low, WH)
    lane = lax.broadcasted_iota(jnp.int32, (288, 288), 1)
    return one_hot(lane == (high * GROUP + step) * WH + row)


def entry_matrix():
    place, chunk = split(line(288, 0), NLON)
    at = chunk * 9 + place
    high, hk = split(at >> 1, WH)
    source = ((high & 1) * 2 + (at & 1)) * 72 + (high >> 1) * WH + hk
    lane = lax.broadcasted_iota(jnp.int32, (288, 288), 1)
    return one_hot(lane == source)


def tables_kernel(spread_ref, rows_ref):
    level, cell = split(line(WTOK, 1), 72)
    col, row = split(cell, WH)
    source = level * HALF_V + row * SPAN + col + (WW - GROUP)
    place = lax.broadcasted_iota(jnp.int32, (LANES_V, WTOK), 0)
    for part in range(PARTS):
        spread_ref[part] = one_hot(place == source - GROUP * part)

    high, low = split(line(SLOTS * 144, 0), 72)
    pair, hk = split(low, WH)
    source = ((pair * 2 + (high & 1)) * WH + hk) * 8 + (high >> 1)
    rows_ref[...] = one_hot(lax.broadcasted_iota(jnp.int32, (SLOTS * 144, 1152), 1) == source)


def make_tables():
    return pl.pallas_call(
        tables_kernel,
        out_shape=(
            jax.ShapeDtypeStruct((PARTS, LANES_V, WTOK), bf16),
            jax.ShapeDtypeStruct((SLOTS * 144, 1152), bf16),
        ),
        out_specs=(vmem(),) * 2,
        compiler_params=params(16),
        cost_estimate=pl.CostEstimate(flops=6000000000, bytes_accessed=20000000, transcendentals=0),
        name="index_tables",
    )()


def layer_norm(x):
    centre = jnp.sum(x, axis=0, keepdims=True) * (1.0 / WIDTH)
    shifted = x - centre
    var = jnp.sum(shifted * shifted, axis=0, keepdims=True) * (1.0 / WIDTH)
    inv = lax.rsqrt(var + epsilon)
    return shifted * inv, inv


def norm_back(normed, inv, grad):
    mean_grad = jnp.sum(grad, axis=0, keepdims=True) * (1.0 / WIDTH)
    mean_proj = jnp.sum(grad * normed, axis=0, keepdims=True) * (1.0 / WIDTH)
    return inv * (grad - mean_grad - normed * mean_proj)


def transpose_into(source_ref, target_ref):
    count = source_ref.shape[1]
    for first in range(0, count, 256):
        size = min(256, count - first)
        target_ref[first : first + size, :] = mm(
            eye(size), source_ref[:, first : first + size], NT
        ).astype(bf16)


def prep_kernel(
    lat_ref,
    band_ref,
    table_ref,
    rows_ref,
    spread_ref,
    bias_ref,
    flat_s,
    line_s,
):
    start, count = my_rows(lat_ref, band_ref)
    slot_of = lax.broadcasted_iota(jnp.int32, (8, 2 * NLAT), 0)
    row_of = lax.broadcasted_iota(jnp.int32, (8, 2 * NLAT), 1)
    flat_s[...] = mm(one_hot((row_of == start + slot_of) & (slot_of < count)), table_ref[...])
    for i in range(144):
        line_s[i * 8 : i * 8 + 8, 0:138] = flat_s[:, 138 * i : 138 * i + 138]
    lines = mm(rows_ref[...], line_s[:, 0:138].astype(bf16))

    regroup = regroup_matrix()
    blank = jnp.zeros((72, HALF_V - 138), f32)
    for slot in range(SLOTS):
        at = slot * 144
        rows = jnp.concatenate([lines[at : at + 72], blank, lines[at + 72 : at + 144], blank], axis=1)
        shifted = [
            rows if step == GROUP - 1 else pltpu.roll(rows, LANES_V - (GROUP - 1 - step), 1)
            for step in range(GROUP)
        ]
        stack = jnp.concatenate(shifted, axis=0).astype(bf16)
        left = mm(regroup, stack).astype(bf16)
        for part in range(PARTS):
            full = mm(left, spread_ref[part])
            for head in range(HEADS):
                for level in range(LEVELS):
                    at = (head * 2 + level) * 24
                    bias_ref[
                        slot,
                        level * 72 + part * 24 : level * 72 + part * 24 + 24,
                        head * WTOK : (head + 1) * WTOK,
                    ] = full[at : at + 24, :]


def diagonal(full):
    return jnp.concatenate(
        [
            full[h * HEAD : (h + 1) * HEAD, h * WTOK : (h + 1) * WTOK]
            for h in range(HEADS)
        ],
        axis=0,
    )


def pack_kernel(order_ref, tok_ref, cot_ref, to_right_ref, to_left_ref):
    cut = (WW - LEFT) * LAT
    for which, ref in ((0, tok_ref), (1, cot_ref)):
        low, high = ref[0].astype(f32), ref[1].astype(f32)
        both = jnp.concatenate([low[cut:], high[cut:]], axis=1)
        to_right_ref[which] = both.astype(bf16)
        both = jnp.concatenate([low[: RIGHT * LAT], high[: RIGHT * LAT]], axis=1)
        to_left_ref[which] = both.astype(bf16)


def my_rows(lat_ref, band_ref):
    lat = lat_ref[0]
    start = jnp.int32(0)
    for i in range(NLAT):
        start = start + jnp.where(i < lat, band_ref[i], 0)
    return start, band_ref[lat]


def early_kernel(
    lat_ref,
    band_ref,
    shift_ref,
    own_t_ref,
    own_c_ref,
    wqkv_ref,
    wproj_ref,
    wup_ref,
    wdown_t_ref,
    x_own_ref,
    c_own_ref,
    sel_l_ref,
    sel_r_ref,
    put_l_ref,
    put_o_ref,
    put_r_ref,
    wqkv_t_ref,
    wproj_t_ref,
    wup_t_ref,
    wdown_ref,
    regroup_ref,
    entry_ref,
):
    regroup_ref[...] = regroup_back_matrix()
    entry_ref[...] = entry_matrix()
    n_left, n_own, n_right = LEFT * LAT, WW * LAT, RIGHT * LAT

    start, count = my_rows(lat_ref, band_ref)
    at = []
    for s in range(SLOTS):
        shift = shift_ref[jnp.minimum(start + s, 2 * NLAT - 1)]
        first = jnp.where(shift <= RIGHT, shift, shift - WW) + LEFT
        at.append(jnp.where(s < count, first * LAT + s * WH, -100000))

    def place(axis):
        shape = (CELL_ROWS, 1) if axis == 0 else (1, CELL_ROWS)
        cell = lax.broadcasted_iota(jnp.int32, shape, axis)
        col = (cell * 43) >> 8
        base = col * LAT + (cell - col * WH)
        return jnp.concatenate([base + at[s] for s in range(SLOTS)], axis=axis)

    goal = place(0)

    def pick(first, count):
        lane = lax.broadcasted_iota(jnp.int32, (288, count), 1)
        return one_hot(goal - first == lane)

    sel_l_ref[...] = pick(0, n_left)
    sel_r_ref[...] = pick(n_left + n_own, n_right)
    sel_o = pick(n_left, n_own)
    for own_ref, into_ref in ((own_t_ref, x_own_ref), (own_c_ref, c_own_ref)):
        for level in range(LEVELS):
            got = mm(sel_o, own_ref[level])
            for slot in range(SLOTS):
                into_ref[slot, level * 72 : level * 72 + 72, :] = got[slot * 72 : slot * 72 + 72]

    goal_t = place(1)

    def put(first, count):
        row = lax.broadcasted_iota(jnp.int32, (count, 288), 0)
        return one_hot(goal_t - first == row)

    put_l_ref[...] = put(0, n_left)
    put_o_ref[...] = put(n_left, n_own)
    put_r_ref[...] = put(n_left + n_own, n_right)

    transpose_into(wqkv_ref, wqkv_t_ref)
    transpose_into(wproj_ref, wproj_t_ref)
    transpose_into(wup_ref, wup_t_ref)
    transpose_into(wdown_t_ref, wdown_ref)


def main_kernel(
    half_ref,
    left_ref,
    right_ref,
    x_own_ref,
    c_own_ref,
    sel_l_ref,
    sel_r_ref,
    put_l_ref,
    put_o_ref,
    put_r_ref,
    bias_ref,
    wqkv_ref,
    wqkv_t_ref,
    wproj_ref,
    wproj_t_ref,
    wup_ref,
    wup_t_ref,
    wdown_ref,
    wdown_t_ref,
    spread_ref,
    regroup_ref,
    entry_ref,
    out_left_ref,
    out_own_ref,
    out_right_ref,
    wsum_ref,
    keep_ref,
    give_ref,
    x_s,
    c_s,
    ro_s,
    rg_s,
    qm_s,
    gm_s,
    acc_s,
    accd_s,
    accq_s,
    ts_s,
    tt_s,
):
    for which, own_ref, scratch in ((0, x_own_ref, x_s), (1, c_own_ref, c_s)):
        edge = mm(sel_l_ref[...], left_ref[which]) + mm(sel_r_ref[...], right_ref[which])
        for level in range(LEVELS):
            for slot in range(SLOTS):
                rows = slice(level * 72, level * 72 + 72)
                scratch[slot, rows, :] = (
                    own_ref[slot, rows, :]
                    + edge[slot * 72 : slot * 72 + 72, level * WIDTH : (level + 1) * WIDTH]
                )

    acc_s[...] = jnp.zeros_like(acc_s)
    accd_s[...] = jnp.zeros_like(accd_s)
    qm_s[...] = jnp.zeros_like(qm_s)
    gm_s[...] = jnp.zeros_like(gm_s)
    tt_s[...] = jnp.zeros_like(tt_s)
    eye_d = eye(WIDTH)
    eye_t = eye(WTOK)
    scale = HEAD ** (-0.5)

    def one_slot(slot):
        x = mm(eye_d, x_s[slot].astype(bf16), NT)
        yield
        cot = mm(eye_d, c_s[slot].astype(bf16), NT)
        yield
        cot_b = cot.astype(bf16)
        na, inv_a = layer_norm(x)
        na_b = na.astype(bf16)
        qkv = mm(wqkv_t_ref[...], na_b)
        yield
        q = (qkv[:WIDTH] * scale).astype(bf16)
        k = qkv[WIDTH : 2 * WIDTH].astype(bf16)
        v = qkv[2 * WIDTH :].astype(bf16)
        k_rows = mm(eye_t, k, NT).astype(bf16)
        yield
        v_rows = mm(eye_t, v, NT).astype(bf16)
        yield
        for h in range(HEADS):
            qm_s[slot, h * HEAD : (h + 1) * HEAD, h * WTOK : (h + 1) * WTOK] = q[
                h * HEAD : (h + 1) * HEAD
            ]
        qm = qm_s[slot]
        scores = mm(k_rows, qm) + bias_ref[slot]
        yield
        top = jnp.max(scores, axis=0, keepdims=True)
        exps = jnp.exp(scores - top)
        probs = exps * (1.0 / jnp.sum(exps, axis=0, keepdims=True))
        probs_b = probs.astype(bf16)
        att_b = diagonal(mm(v, probs_b)).astype(bf16)
        yield
        hidden = x + mm(wproj_t_ref[...], att_b)
        yield
        nb, inv_b = layer_norm(hidden)
        nb_b = nb.astype(bf16)
        pre = mm(wup_t_ref[...], nb_b)
        yield
        cdf = 0.5 * (1.0 + lax.erf(pre * 0.7071067811865476))
        density = jnp.exp(-0.5 * pre * pre) * 0.3989422804014327
        act_b = (pre * cdf).astype(bf16)
        slope = cdf + pre * density
        out = hidden + mm(wdown_t_ref[...], act_b)
        yield
        ro_s[slot] = mm(eye_t, out.astype(bf16), NT)
        yield
        gpre_b = (mm(wdown_ref[...], cot_b) * slope).astype(bf16)
        yield
        accd_s[...] += mm(act_b, cot_b, NT)
        yield
        gh = cot + norm_back(nb, inv_b, mm(wup_ref[...], gpre_b))
        yield
        gh_b = gh.astype(bf16)
        acc_s[:, 768:1536] += mm(nb_b, gpre_b, NT)
        yield
        acc_s[:, 576:768] += mm(att_b, gh_b, NT)
        yield
        ga = mm(wproj_ref[...], gh_b).astype(bf16)
        yield
        for h in range(HEADS):
            gm_s[slot, h * HEAD : (h + 1) * HEAD, h * WTOK : (h + 1) * WTOK] = ga[
                h * HEAD : (h + 1) * HEAD
            ]
        gm = gm_s[slot]
        gp = mm(v_rows, gm)
        yield
        gs = probs * (gp - jnp.sum(probs * gp, axis=0, keepdims=True))
        gs_b = gs.astype(bf16)
        gq = diagonal(mm(k, gs_b)) * scale
        yield
        gk = mm(qm, gs_b, NT)
        yield
        gv = mm(gm, probs_b, NT)
        yield
        gc_b = jnp.concatenate([gq, gk, gv], axis=0).astype(bf16)
        acc_s[:, 0:576] += mm(na_b, gc_b, NT)
        yield
        gt = gh + norm_back(na, inv_a, mm(wqkv_ref[...], gc_b))
        yield
        rg_s[slot] = mm(eye_t, gt.astype(bf16), NT)
        yield

        heads = [gs[:, h * WTOK : (h + 1) * WTOK] for h in range(HEADS)]
        total = None
        for part in range(PARTS):
            rows = jnp.concatenate(
                [
                    piece[level * 72 + part * 24 : level * 72 + part * 24 + 24]
                    for piece in heads
                    for level in range(LEVELS)
                ],
                axis=0,
            ).astype(bf16)
            term = mm(rows, spread_ref[part], NT)
            total = term if total is None else total + term
            yield
        steps = mm(regroup_ref[...], total.astype(bf16))
        yield
        table = steps[216:288]
        for step in range(GROUP - 1):
            table = table + pltpu.roll(steps[step * 72 : step * 72 + 72], GROUP - 1 - step, 1)
        for piece, first in enumerate((0, 69, HALF_V, HALF_V + 69)):
            ts_s[slot, piece * 72 : piece * 72 + 72, 0:69] = table[:, first : first + 69]

    for first in range(0, SLOTS, 4):
        runs = [one_slot(slot) for slot in range(first, first + 4)]
        while runs:
            runs = [run for run in runs if next(run, run) is not run]

    for slot in range(SLOTS):
        values = ts_s[slot][:, 0:69].astype(bf16)
        entries = mm(entry_ref[...], values)
        for n in range(9):
            tt_s[pl.ds(slot * 9 + n, NLON, stride=PER_Z), 0:69] = entries[
                n * NLON : (n + 1) * NLON
            ]
    size = Z * PER_Z
    half = half_ref[0]
    mine = tt_s[pl.ds(pl.multiple_of(half * size, 8), size), :]
    keep_ref[...] = mine.reshape(Z, PER_Z, 128).astype(bf16)
    other = tt_s[pl.ds(pl.multiple_of((1 - half) * size, 8), size), :]
    give_ref[...] = other.reshape(Z, PER_Z, 128).astype(bf16)

    for x in range(2):
        accq_s[:, x * 384 : x * 384 + 288] = acc_s[:, x * 288 : x * 288 + 288]
        accq_s[:, x * 384 + 288 : x * 384 + 384] = acc_s[:, 576 + x * 96 : 576 + x * 96 + 96]
    for x in range(2):
        for i in range(NLAT):
            top = accq_s[12 * i : 12 * i + 12, x * 384 : x * 384 + 384]
            low = acc_s[12 * i : 12 * i + 12, 768 + x * 384 : 768 + x * 384 + 384]
            down = [
                accd_s[48 * i + g * 24 : 48 * i + g * 24 + 24, x * 96 : x * 96 + 96]
                for g in range(2)
            ]
            both = jnp.concatenate([top, low], axis=0)
            wsum_ref[x * NLAT + i] = jnp.concatenate([both] + down, axis=1).astype(bf16)

    for which, scratch in ((0, ro_s), (1, rg_s)):
        levels = [
            jnp.concatenate(
                [scratch[slot, level * 72 : level * 72 + 72] for slot in range(SLOTS)], axis=0
            )
            for level in range(LEVELS)
        ]
        for level in range(LEVELS):
            out_own_ref[which, level] = mm(put_o_ref[...], levels[level].astype(bf16)).astype(bf16)
        rows = jnp.concatenate(levels, axis=1).astype(bf16)
        out_left_ref[which] = mm(put_l_ref[...], rows).astype(bf16)
        out_right_ref[which] = mm(put_r_ref[...], rows).astype(bf16)


def mid_kernel(
    w_ref,
    keep_ref,
    got_ref,
    out_ref,
):
    total = w_ref[0].astype(f32)
    for i in range(1, 2 * NLAT):
        total = total + w_ref[i].astype(f32)
    qkv, proj = total[0:12, 0:288], total[0:12, 288:384]
    up = total[12:24, 0:384]
    down = [
        total[0:12, 384:480],
        total[12:24, 384:480],
        total[0:12, 480:576],
        total[12:24, 480:576],
    ]
    for z in range(Z):
        part = jnp.concatenate(
            [
                jnp.concatenate(
                    [qkv[:, 18 * z : 18 * z + 18], proj[:, 6 * z : 6 * z + 6]], axis=1
                ),
                up[:, 24 * z : 24 * z + 24],
                jnp.concatenate([piece[:, 6 * z : 6 * z + 6] for piece in down], axis=1),
            ],
            axis=0,
        )
        table = keep_ref[z, :, 0:69].astype(f32) + got_ref[z, :, 0:69].astype(f32)
        rest = jnp.concatenate(
            [
                jnp.concatenate([table[32:36, 23 * n : 23 * n + 23] for n in range(3)], axis=0),
                part[32:36, 0:23],
            ],
            axis=0,
        )
        rest = jnp.concatenate([rest, jnp.zeros((SEND - 16, 23), f32)], axis=0)
        last = jnp.concatenate([jnp.zeros((12, 1), f32), part[32:36, 23:24]], axis=0)
        last = jnp.concatenate([last, jnp.zeros((SEND - 16, 1), f32)], axis=0)
        out_ref[z] = jnp.concatenate(
            [table[0:SEND], part[0:SEND], rest, last, jnp.zeros((SEND, 11), f32)], axis=1
        ).astype(bf16)


def cells_kernel(own_ref, from_left_ref, from_right_ref, cells_ref, grad_ref):
    for which, ref in ((0, cells_ref), (1, grad_ref)):
        for level in range(LEVELS):
            lanes = slice(level * WIDTH, (level + 1) * WIDTH)
            own = own_ref[which, level].astype(f32)
            first, last = from_left_ref[which], from_right_ref[which]
            near, far = RIGHT * LAT, (WW - LEFT) * LAT
            ref[level] = jnp.concatenate(
                [
                    own[:near] + first.astype(f32)[:, lanes],
                    own[near:far],
                    own[far:] + last.astype(f32)[:, lanes],
                ],
                axis=0,
            ).astype(bf16)


def fin_kernel(scale, lat_ref, band_ref, in_ref, qkv_ref, proj_ref, up_ref, down_ref, route_ref):
    total = in_ref[0].astype(f32)
    for i in range(1, Z):
        total = total + in_ref[i].astype(f32)
    extra = jnp.concatenate([total[4 * n : 4 * n + 4, 93:116] for n in range(3)], axis=1)
    extra = jnp.concatenate([extra, total[12:16, 93:117], jnp.zeros((4, 35), f32)], axis=1)
    total = jnp.concatenate([total, extra], axis=0)
    qkv_ref[...] = total[0:12, 69:87] * scale
    proj_ref[...] = total[0:12, 87:93] * scale
    up_ref[...] = total[12:24, 69:93] * scale
    down_ref[...] = (
        jnp.concatenate([total[24:36, 69 + 6 * g : 75 + 6 * g] for g in range(4)], axis=0) * scale
    )
    table = total[0:36].astype(bf16)
    start, count = my_rows(lat_ref, band_ref)
    spot = line(NLAT * 32, 0)
    row, place = spot >> 4, spot & 15
    live = (row >= start) & (row < start + count) & (place < 9)
    wanted = jnp.where(live, (row - start) * 9 + place, -1)
    hits = one_hot(lax.broadcasted_iota(jnp.int32, (NLAT * 32, 36), 1) == wanted)
    route_ref[...] = mm(hits, table).reshape(NLAT, 32, 128).astype(bf16)


def table_kernel(in_ref, out_ref):
    total = in_ref[0].astype(f32)
    for i in range(1, NLAT):
        total = total + in_ref[i].astype(f32)
    for j in range(2):
        out_ref[j : j + 1, :] = jnp.concatenate(
            [total[j * 16 + n : j * 16 + n + 1, 0:69] for n in range(9)], axis=1
        )


def vmem():
    return pl.BlockSpec(memory_space=pltpu.VMEM)


def smem():
    return pl.BlockSpec(memory_space=pltpu.SMEM)


def params(mib):
    return pltpu.CompilerParams(vmem_limit_bytes=mib * 1024 * 1024)


def to_lon(x, by):
    count = lax.axis_size("lon")
    return lax.ppermute(x, "lon", [(i, (i + by) % count) for i in range(count)])


def prepare(lat, band_rows, bias_table, tables):
    return pl.pallas_call(
        prep_kernel,
        out_shape=jax.ShapeDtypeStruct((SLOTS, WTOK, ALL_Q), f32),
        in_specs=[smem()] * 2 + [vmem()] * 3,
        out_specs=vmem(),
        scratch_shapes=[pltpu.VMEM((8, HEADS * POS), f32), pltpu.VMEM((1152, HALF_V), f32)],
        compiler_params=params(24),
        cost_estimate=pl.CostEstimate(flops=1000000000, bytes_accessed=6000000, transcendentals=0),
        name="prepare",
    )(lat, band_rows, bias_table, *tables)


def early_part(lat, band_rows, lon_shift, own_t, own_c, w_qkv, w_proj, w_up, w_down_t):
    windows = jax.ShapeDtypeStruct((SLOTS, WTOK, WIDTH), f32)
    n_left, n_own, n_right = LEFT * LAT, WW * LAT, RIGHT * LAT
    shapes = ((288, n_left), (288, n_right), (n_left, 288), (n_own, 288), (n_right, 288))
    flips = ((3 * WIDTH, WIDTH), (WIDTH, WIDTH), (HID, WIDTH), (HID, WIDTH))
    flips = flips + ((288, 288), (288, 288))
    return pl.pallas_call(
        early_kernel,
        out_shape=(windows, windows)
        + tuple(jax.ShapeDtypeStruct(shape, bf16) for shape in shapes + flips),
        in_specs=[smem()] * 3 + [vmem()] * 6,
        out_specs=(vmem(),) * 13,
        compiler_params=params(24),
        cost_estimate=pl.CostEstimate(flops=1000000000, bytes_accessed=6000000, transcendentals=0),
        name="own_cells",
    )(lat, band_rows, lon_shift, own_t, own_c, w_qkv, w_proj, w_up, w_down_t)


def block_pass(half, left, right, early, bias, weights, tables):
    return pl.pallas_call(
        main_kernel,
        out_shape=(
            jax.ShapeDtypeStruct((2, LEFT * LAT, 2 * WIDTH), bf16),
            jax.ShapeDtypeStruct((2, LEVELS, WW * LAT, WIDTH), bf16),
            jax.ShapeDtypeStruct((2, RIGHT * LAT, 2 * WIDTH), bf16),
            jax.ShapeDtypeStruct((2 * NLAT, 24, 576), bf16),
            jax.ShapeDtypeStruct((Z, PER_Z, 128), bf16),
            jax.ShapeDtypeStruct((Z, PER_Z, 128), bf16),
        ),
        in_specs=[smem()] + [vmem()] * 21,
        out_specs=(vmem(),) * 6,
        scratch_shapes=[
            pltpu.VMEM((SLOTS, WTOK, WIDTH), f32),
            pltpu.VMEM((SLOTS, WTOK, WIDTH), f32),
            pltpu.VMEM((SLOTS, WTOK, WIDTH), f32),
            pltpu.VMEM((SLOTS, WTOK, WIDTH), f32),
            pltpu.VMEM((SLOTS, WIDTH, ALL_Q), bf16),
            pltpu.VMEM((SLOTS, WIDTH, ALL_Q), bf16),
            pltpu.VMEM((WIDTH, 1536), f32),
            pltpu.VMEM((HID, WIDTH), f32),
            pltpu.VMEM((WIDTH, 768), f32),
            pltpu.VMEM((SLOTS, 288, 128), f32),
            pltpu.VMEM((NLON * PER_Z, 128), f32),
        ],
        compiler_params=params(32),
        name="block_pass",
    )(half, left, right, *early, bias, *weights, *tables)


def local(tokens, cotangent, w_qkv, w_proj, w_up, w_down, bias_table, band_rows, lon_shift):
    latwin = bias_table.shape[0]
    lat = lax.axis_index("lat").reshape(1)
    half = (lax.axis_index("lon") // Z).reshape(1)

    own_t = tokens.transpose(0, 2, 1, 3).reshape(LEVELS, WW * LAT, WIDTH)
    own_c = cotangent.transpose(0, 2, 1, 3).reshape(LEVELS, WW * LAT, WIDTH)
    spread, rows = make_tables()
    to_right, to_left = pl.pallas_call(
        pack_kernel,
        out_shape=(
            jax.ShapeDtypeStruct((2, LEFT * LAT, 2 * WIDTH), bf16),
            jax.ShapeDtypeStruct((2, RIGHT * LAT, 2 * WIDTH), bf16),
        ),
        in_specs=[pl.BlockSpec(memory_space=pl.ANY)] + [vmem()] * 2,
        out_specs=(vmem(),) * 2,
        compiler_params=params(16),
        name="pack_edges",
    )(rows, own_t, own_c)
    left = to_lon(to_right, 1)
    right = to_lon(to_left, -1)

    bias = prepare(lat, band_rows, bias_table, (rows, spread))
    w_down_t = w_down.T
    early = early_part(
        lat, band_rows, lon_shift, own_t, own_c, w_qkv, w_proj, w_up, w_down_t
    )
    flip = early[7:]
    weights = (w_qkv, flip[0], w_proj, flip[1], w_up, flip[2], flip[3], w_down_t)
    out_left, out_own, out_right, w_sums, t_keep, t_give = block_pass(
        half, left, right, early[:7], bias, weights, (spread, flip[4], flip[5])
    )

    t_got = to_lon(t_give, Z)
    from_right = to_lon(out_left, -1)
    from_left = to_lon(out_right, 1)
    near = [[(x * Z + z) * NLAT + i for x in range(2) for i in range(NLAT)] for z in range(Z)]
    ring = [[x * Z + z for z in range(Z)] for x in range(2)]
    w_got = lax.all_to_all(w_sums, ("lon", "lat"), 0, 0, axis_index_groups=near)
    cells_shape = jax.ShapeDtypeStruct((LEVELS, WW * LAT, WIDTH), bf16)
    lon_send = pl.pallas_call(
        mid_kernel,
        out_shape=jax.ShapeDtypeStruct((Z, SEND, 128), bf16),
        in_specs=[vmem()] * 3,
        out_specs=vmem(),
        compiler_params=params(24),
        name="sum_lat",
    )(w_got, t_keep, t_got)
    lon_send, from_left, from_right = lax.optimization_barrier(
        (lon_send, from_left, from_right)
    )
    cells, grads = pl.pallas_call(
        cells_kernel,
        out_shape=(cells_shape, cells_shape),
        in_specs=[vmem()] * 3,
        out_specs=(vmem(),) * 2,
        compiler_params=params(16),
        cost_estimate=pl.CostEstimate(flops=100000000, bytes_accessed=3000000, transcendentals=0),
        name="join_cells",
    )(out_own, from_left, from_right)
    output = cells.reshape(LEVELS, WW, LAT, WIDTH).transpose(0, 2, 1, 3)
    grad_tokens = grads.reshape(LEVELS, WW, LAT, WIDTH).transpose(0, 2, 1, 3)

    lon_got = lax.all_to_all(lon_send, "lon", 0, 0, axis_index_groups=ring)
    scale_grad = float(latwin * WH * LEVELS * WW * NLON) ** (-0.5)
    grad_qkv, grad_proj, grad_up, grad_down, route = pl.pallas_call(
        functools.partial(fin_kernel, scale_grad),
        out_shape=(
            jax.ShapeDtypeStruct((12, 18), f32),
            jax.ShapeDtypeStruct((12, 6), f32),
            jax.ShapeDtypeStruct((12, 24), f32),
            jax.ShapeDtypeStruct((48, 6), f32),
            jax.ShapeDtypeStruct((NLAT, 32, 128), bf16),
        ),
        in_specs=[smem(), smem(), vmem()],
        out_specs=(vmem(),) * 5,
        compiler_params=params(24),
        name="sum_lon",
    )(lat, band_rows, lon_got)
    route_got = lax.all_to_all(route, "lat", 0, 0)
    grad_table = pl.pallas_call(
        table_kernel,
        out_shape=jax.ShapeDtypeStruct((2, 621), f32),
        in_specs=[vmem()],
        out_specs=vmem(),
        compiler_params=params(24),
        name="sum_table",
    )(route_got)
    return (output, grad_tokens, grad_qkv, grad_proj, grad_up, grad_down, grad_table)


def solution(mesh):
    grid = P(None, "lat", "lon", None)
    cut = P("lat", "lon")
    return jax.shard_map(
        local,
        mesh=mesh,
        in_specs=(grid, grid, P(), P(), P(), P(), P(), P(), P()),
        out_specs=(grid, grid, cut, cut, cut, cut, cut),
        check_vma=False,
    )
```

```python
import functools

import jax
import jax.numpy as jnp
from jax import lax
from jax.experimental import pallas as pl
from jax.experimental.pallas import tpu as pltpu
from jax.sharding import PartitionSpec as P

HEADS = 6
HEAD = 32
WIDTH = 192
HID = 768
WH = 6
WW = 12
LEVELS = 2
SLOTS = 4
WTOK = 144
CELL_ROWS = 72
POS = 3312
SPAN = 23
LEFT = 5
RIGHT = 6
LAT = 24
NLAT = 16
NLON = 32
ALL_Q = HEADS * WTOK
GROUP = 4
PARTS = WW // GROUP
LANES_V = 512
HALF_V = 256
Z = 16
PER_Z = 40
SEND = 32

bf16 = jnp.bfloat16
f32 = jnp.float32
epsilon = 1e-05

NN = (((1,), (0,)), ((), ()))
NT = (((1,), (1,)), ((), ()))


def mm(left, right, dims=NN):
    return lax.dot_general(left, right, dims, preferred_element_type=f32)


def one_hot(condition):
    return jnp.where(condition, 1.0, 0.0).astype(bf16)


def eye(count):
    rows = lax.broadcasted_iota(jnp.int32, (count, count), 0)
    cols = lax.broadcasted_iota(jnp.int32, (count, count), 1)
    return one_hot(rows == cols)


def split(x, size):
    high = (x * ((65536 + size - 1) // size)) >> 16
    return high, x - high * size


def line(count, axis):
    shape = (count, 1) if axis == 0 else (1, count)
    return lax.broadcasted_iota(jnp.int32, shape, axis)


def regroup_matrix():
    high, low = split(line(288, 0), 24)
    step, row = split(low, WH)
    lane = lax.broadcasted_iota(jnp.int32, (288, 288), 1)
    return one_hot(lane == step * 72 + high * WH + row)


def regroup_back_matrix():
    step, low = split(line(288, 0), 72)
    high, row = split(low, WH)
    lane = lax.broadcasted_iota(jnp.int32, (288, 288), 1)
    return one_hot(lane == (high * GROUP + step) * WH + row)


def entry_matrix():
    place, chunk = split(line(288, 0), NLON)
    at = chunk * 9 + place
    high, hk = split(at >> 1, WH)
    source = ((high & 1) * 2 + (at & 1)) * 72 + (high >> 1) * WH + hk
    lane = lax.broadcasted_iota(jnp.int32, (288, 288), 1)
    return one_hot(lane == source)


def tables_kernel(spread_ref, rows_ref):
    level, cell = split(line(WTOK, 1), 72)
    col, row = split(cell, WH)
    source = level * HALF_V + row * SPAN + col + (WW - GROUP)
    place = lax.broadcasted_iota(jnp.int32, (LANES_V, WTOK), 0)
    for part in range(PARTS):
        spread_ref[part] = one_hot(place == source - GROUP * part)

    high, low = split(line(SLOTS * 144, 0), 72)
    pair, hk = split(low, WH)
    source = ((pair * 2 + (high & 1)) * WH + hk) * 8 + (high >> 1)
    rows_ref[...] = one_hot(lax.broadcasted_iota(jnp.int32, (SLOTS * 144, 1152), 1) == source)


def make_tables():
    return pl.pallas_call(
        tables_kernel,
        out_shape=(
            jax.ShapeDtypeStruct((PARTS, LANES_V, WTOK), bf16),
            jax.ShapeDtypeStruct((SLOTS * 144, 1152), bf16),
        ),
        out_specs=(vmem(),) * 2,
        compiler_params=params(16),
        cost_estimate=pl.CostEstimate(flops=6000000000, bytes_accessed=20000000, transcendentals=0),
        name="index_tables",
    )()


def layer_norm(x):
    centre = jnp.sum(x, axis=0, keepdims=True) * (1.0 / WIDTH)
    shifted = x - centre
    var = jnp.sum(shifted * shifted, axis=0, keepdims=True) * (1.0 / WIDTH)
    inv = lax.rsqrt(var + epsilon)
    return shifted * inv, inv


def norm_back(normed, inv, grad):
    mean_grad = jnp.sum(grad, axis=0, keepdims=True) * (1.0 / WIDTH)
    mean_proj = jnp.sum(grad * normed, axis=0, keepdims=True) * (1.0 / WIDTH)
    return inv * (grad - mean_grad - normed * mean_proj)


def transpose_into(source_ref, target_ref):
    count = source_ref.shape[1]
    for first in range(0, count, 256):
        size = min(256, count - first)
        target_ref[first : first + size, :] = mm(
            eye(size), source_ref[:, first : first + size], NT
        ).astype(bf16)


def prep_kernel(
    lat_ref,
    band_ref,
    table_ref,
    rows_ref,
    spread_ref,
    bias_ref,
    flat_s,
    line_s,
):
    start, count = my_rows(lat_ref, band_ref)
    slot_of = lax.broadcasted_iota(jnp.int32, (8, 2 * NLAT), 0)
    row_of = lax.broadcasted_iota(jnp.int32, (8, 2 * NLAT), 1)
    flat_s[...] = mm(one_hot((row_of == start + slot_of) & (slot_of < count)), table_ref[...])
    for i in range(144):
        line_s[i * 8 : i * 8 + 8, 0:138] = flat_s[:, 138 * i : 138 * i + 138]
    lines = mm(rows_ref[...], line_s[:, 0:138].astype(bf16))

    regroup = regroup_matrix()
    blank = jnp.zeros((72, HALF_V - 138), f32)
    for slot in range(SLOTS):
        at = slot * 144
        rows = jnp.concatenate([lines[at : at + 72], blank, lines[at + 72 : at + 144], blank], axis=1)
        shifted = [
            rows if step == GROUP - 1 else pltpu.roll(rows, LANES_V - (GROUP - 1 - step), 1)
            for step in range(GROUP)
        ]
        stack = jnp.concatenate(shifted, axis=0).astype(bf16)
        left = mm(regroup, stack).astype(bf16)
        for part in range(PARTS):
            full = mm(left, spread_ref[part])
            for head in range(HEADS):
                for level in range(LEVELS):
                    at = (head * 2 + level) * 24
                    bias_ref[
                        slot,
                        level * 72 + part * 24 : level * 72 + part * 24 + 24,
                        head * WTOK : (head + 1) * WTOK,
                    ] = full[at : at + 24, :]


def diagonal(full):
    return jnp.concatenate(
        [
            full[h * HEAD : (h + 1) * HEAD, h * WTOK : (h + 1) * WTOK]
            for h in range(HEADS)
        ],
        axis=0,
    )


def pack_kernel(order_ref, tok_ref, cot_ref, to_right_ref, to_left_ref):
    cut = (WW - LEFT) * LAT
    for which, ref in ((0, tok_ref), (1, cot_ref)):
        low, high = ref[0].astype(f32), ref[1].astype(f32)
        both = jnp.concatenate([low[cut:], high[cut:]], axis=1)
        to_right_ref[which] = both.astype(bf16)
        both = jnp.concatenate([low[: RIGHT * LAT], high[: RIGHT * LAT]], axis=1)
        to_left_ref[which] = both.astype(bf16)


def my_rows(lat_ref, band_ref):
    lat = lat_ref[0]
    start = jnp.int32(0)
    for i in range(NLAT):
        start = start + jnp.where(i < lat, band_ref[i], 0)
    return start, band_ref[lat]


def early_kernel(
    lat_ref,
    band_ref,
    shift_ref,
    own_t_ref,
    own_c_ref,
    wqkv_ref,
    wproj_ref,
    wup_ref,
    wdown_t_ref,
    x_own_ref,
    c_own_ref,
    sel_l_ref,
    sel_r_ref,
    put_l_ref,
    put_o_ref,
    put_r_ref,
    wqkv_t_ref,
    wproj_t_ref,
    wup_t_ref,
    wdown_ref,
    regroup_ref,
    entry_ref,
):
    regroup_ref[...] = regroup_back_matrix()
    entry_ref[...] = entry_matrix()
    n_left, n_own, n_right = LEFT * LAT, WW * LAT, RIGHT * LAT

    start, count = my_rows(lat_ref, band_ref)
    at = []
    for s in range(SLOTS):
        shift = shift_ref[jnp.minimum(start + s, 2 * NLAT - 1)]
        first = jnp.where(shift <= RIGHT, shift, shift - WW) + LEFT
        at.append(jnp.where(s < count, first * LAT + s * WH, -100000))

    def place(axis):
        shape = (CELL_ROWS, 1) if axis == 0 else (1, CELL_ROWS)
        cell = lax.broadcasted_iota(jnp.int32, shape, axis)
        col = (cell * 43) >> 8
        base = col * LAT + (cell - col * WH)
        return jnp.concatenate([base + at[s] for s in range(SLOTS)], axis=axis)

    goal = place(0)

    def pick(first, count):
        lane = lax.broadcasted_iota(jnp.int32, (288, count), 1)
        return one_hot(goal - first == lane)

    sel_l_ref[...] = pick(0, n_left)
    sel_r_ref[...] = pick(n_left + n_own, n_right)
    sel_o = pick(n_left, n_own)
    for own_ref, into_ref in ((own_t_ref, x_own_ref), (own_c_ref, c_own_ref)):
        for level in range(LEVELS):
            got = mm(sel_o, own_ref[level])
            for slot in range(SLOTS):
                into_ref[slot, level * 72 : level * 72 + 72, :] = got[slot * 72 : slot * 72 + 72]

    goal_t = place(1)

    def put(first, count):
        row = lax.broadcasted_iota(jnp.int32, (count, 288), 0)
        return one_hot(goal_t - first == row)

    put_l_ref[...] = put(0, n_left)
    put_o_ref[...] = put(n_left, n_own)
    put_r_ref[...] = put(n_left + n_own, n_right)

    transpose_into(wqkv_ref, wqkv_t_ref)
    transpose_into(wproj_ref, wproj_t_ref)
    transpose_into(wup_ref, wup_t_ref)
    transpose_into(wdown_t_ref, wdown_ref)


def main_kernel(
    half_ref,
    left_ref,
    right_ref,
    x_own_ref,
    c_own_ref,
    sel_l_ref,
    sel_r_ref,
    put_l_ref,
    put_o_ref,
    put_r_ref,
    bias_ref,
    wqkv_ref,
    wqkv_t_ref,
    wproj_ref,
    wproj_t_ref,
    wup_ref,
    wup_t_ref,
    wdown_ref,
    wdown_t_ref,
    spread_ref,
    regroup_ref,
    entry_ref,
    out_left_ref,
    out_own_ref,
    out_right_ref,
    wsum_ref,
    keep_ref,
    give_ref,
    x_s,
    c_s,
    ro_s,
    rg_s,
    qm_s,
    gm_s,
    acc_s,
    accd_s,
    accq_s,
    ts_s,
    tt_s,
):
    for which, own_ref, scratch in ((0, x_own_ref, x_s), (1, c_own_ref, c_s)):
        edge = mm(sel_l_ref[...], left_ref[which]) + mm(sel_r_ref[...], right_ref[which])
        for level in range(LEVELS):
            for slot in range(SLOTS):
                rows = slice(level * 72, level * 72 + 72)
                scratch[slot, rows, :] = (
                    own_ref[slot, rows, :]
                    + edge[slot * 72 : slot * 72 + 72, level * WIDTH : (level + 1) * WIDTH]
                )

    acc_s[...] = jnp.zeros_like(acc_s)
    accd_s[...] = jnp.zeros_like(accd_s)
    qm_s[...] = jnp.zeros_like(qm_s)
    gm_s[...] = jnp.zeros_like(gm_s)
    tt_s[...] = jnp.zeros_like(tt_s)
    eye_d = eye(WIDTH)
    eye_t = eye(WTOK)
    scale = HEAD ** (-0.5)

    def one_slot(slot):
        x = mm(eye_d, x_s[slot].astype(bf16), NT)
        yield
        cot = mm(eye_d, c_s[slot].astype(bf16), NT)
        yield
        cot_b = cot.astype(bf16)
        na, inv_a = layer_norm(x)
        na_b = na.astype(bf16)
        qkv = mm(wqkv_t_ref[...], na_b)
        yield
        q = (qkv[:WIDTH] * scale).astype(bf16)
        k = qkv[WIDTH : 2 * WIDTH].astype(bf16)
        v = qkv[2 * WIDTH :].astype(bf16)
        k_rows = mm(eye_t, k, NT).astype(bf16)
        yield
        v_rows = mm(eye_t, v, NT).astype(bf16)
        yield
        for h in range(HEADS):
            qm_s[slot, h * HEAD : (h + 1) * HEAD, h * WTOK : (h + 1) * WTOK] = q[
                h * HEAD : (h + 1) * HEAD
            ]
        qm = qm_s[slot]
        scores = mm(k_rows, qm) + bias_ref[slot]
        yield
        top = jnp.max(scores, axis=0, keepdims=True)
        exps = jnp.exp(scores - top)
        probs = exps * (1.0 / jnp.sum(exps, axis=0, keepdims=True))
        probs_b = probs.astype(bf16)
        att_b = diagonal(mm(v, probs_b)).astype(bf16)
        yield
        hidden = x + mm(wproj_t_ref[...], att_b)
        yield
        nb, inv_b = layer_norm(hidden)
        nb_b = nb.astype(bf16)
        pre = mm(wup_t_ref[...], nb_b)
        yield
        cdf = 0.5 * (1.0 + lax.erf(pre * 0.7071067811865476))
        density = jnp.exp(-0.5 * pre * pre) * 0.3989422804014327
        act_b = (pre * cdf).astype(bf16)
        slope = cdf + pre * density
        out = hidden + mm(wdown_t_ref[...], act_b)
        yield
        ro_s[slot] = mm(eye_t, out.astype(bf16), NT)
        yield
        gpre_b = (mm(wdown_ref[...], cot_b) * slope).astype(bf16)
        yield
        accd_s[...] += mm(act_b, cot_b, NT)
        yield
        gh = cot + norm_back(nb, inv_b, mm(wup_ref[...], gpre_b))
        yield
        gh_b = gh.astype(bf16)
        acc_s[:, 768:1536] += mm(nb_b, gpre_b, NT)
        yield
        acc_s[:, 576:768] += mm(att_b, gh_b, NT)
        yield
        ga = mm(wproj_ref[...], gh_b).astype(bf16)
        yield
        for h in range(HEADS):
            gm_s[slot, h * HEAD : (h + 1) * HEAD, h * WTOK : (h + 1) * WTOK] = ga[
                h * HEAD : (h + 1) * HEAD
            ]
        gm = gm_s[slot]
        gp = mm(v_rows, gm)
        yield
        gs = probs * (gp - jnp.sum(probs * gp, axis=0, keepdims=True))
        gs_b = gs.astype(bf16)
        gq = diagonal(mm(k, gs_b)) * scale
        yield
        gk = mm(qm, gs_b, NT)
        yield
        gv = mm(gm, probs_b, NT)
        yield
        gc_b = jnp.concatenate([gq, gk, gv], axis=0).astype(bf16)
        acc_s[:, 0:576] += mm(na_b, gc_b, NT)
        yield
        gt = gh + norm_back(na, inv_a, mm(wqkv_ref[...], gc_b))
        yield
        rg_s[slot] = mm(eye_t, gt.astype(bf16), NT)
        yield

        heads = [gs[:, h * WTOK : (h + 1) * WTOK] for h in range(HEADS)]
        total = None
        for part in range(PARTS):
            rows = jnp.concatenate(
                [
                    piece[level * 72 + part * 24 : level * 72 + part * 24 + 24]
                    for piece in heads
                    for level in range(LEVELS)
                ],
                axis=0,
            ).astype(bf16)
            term = mm(rows, spread_ref[part], NT)
            total = term if total is None else total + term
            yield
        steps = mm(regroup_ref[...], total.astype(bf16))
        yield
        table = steps[216:288]
        for step in range(GROUP - 1):
            table = table + pltpu.roll(steps[step * 72 : step * 72 + 72], GROUP - 1 - step, 1)
        for piece, first in enumerate((0, 69, HALF_V, HALF_V + 69)):
            ts_s[slot, piece * 72 : piece * 72 + 72, 0:69] = table[:, first : first + 69]

    for first in range(0, SLOTS, 4):
        runs = [one_slot(slot) for slot in range(first, first + 4)]
        while runs:
            runs = [run for run in runs if next(run, run) is not run]

    for slot in range(SLOTS):
        values = ts_s[slot][:, 0:69].astype(bf16)
        entries = mm(entry_ref[...], values)
        for n in range(9):
            tt_s[pl.ds(slot * 9 + n, NLON, stride=PER_Z), 0:69] = entries[
                n * NLON : (n + 1) * NLON
            ]
    size = Z * PER_Z
    half = half_ref[0]
    mine = tt_s[pl.ds(pl.multiple_of(half * size, 8), size), :]
    keep_ref[...] = mine.reshape(Z, PER_Z, 128).astype(bf16)
    other = tt_s[pl.ds(pl.multiple_of((1 - half) * size, 8), size), :]
    give_ref[...] = mm(eye(80), other[:, 0:80].astype(bf16), NT).astype(bf16)

    for x in range(2):
        accq_s[:, x * 384 : x * 384 + 288] = acc_s[:, x * 288 : x * 288 + 288]
        accq_s[:, x * 384 + 288 : x * 384 + 384] = acc_s[:, 576 + x * 96 : 576 + x * 96 + 96]
    for x in range(2):
        for i in range(NLAT):
            top = accq_s[12 * i : 12 * i + 12, x * 384 : x * 384 + 384]
            low = acc_s[12 * i : 12 * i + 12, 768 + x * 384 : 768 + x * 384 + 384]
            down = [
                accd_s[48 * i + g * 24 : 48 * i + g * 24 + 24, x * 96 : x * 96 + 96]
                for g in range(2)
            ]
            both = jnp.concatenate([top, low], axis=0)
            both = jnp.concatenate([both] + down, axis=1)
            wsum_ref[x * NLAT + i] = jnp.concatenate(
                [both[:, 128 * n : 128 * n + 128] for n in range(4)]
                + [
                    jnp.concatenate([both[0:12, 512:576], both[12:24, 512:576]], axis=1),
                    jnp.zeros((4, 128), f32),
                ],
                axis=0,
            ).astype(bf16)

    for which, scratch in ((0, ro_s), (1, rg_s)):
        levels = [
            jnp.concatenate(
                [scratch[slot, level * 72 : level * 72 + 72] for slot in range(SLOTS)], axis=0
            )
            for level in range(LEVELS)
        ]
        for level in range(LEVELS):
            out_own_ref[which, level] = mm(put_o_ref[...], levels[level].astype(bf16)).astype(bf16)
        rows = jnp.concatenate(levels, axis=1).astype(bf16)
        out_left_ref[which] = mm(put_l_ref[...], rows).astype(bf16)
        out_right_ref[which] = mm(put_r_ref[...], rows).astype(bf16)


def mid_kernel(
    w_ref,
    keep_ref,
    got_ref,
    out_ref,
):
    total = w_ref[0].astype(f32)
    for i in range(1, 2 * NLAT):
        total = total + w_ref[i].astype(f32)
    half = jnp.concatenate([total[96:108, 0:64], total[96:108, 64:128]], axis=0)
    total = jnp.concatenate([total[24 * n : 24 * n + 24] for n in range(4)] + [half], axis=1)
    got = got_ref[...]
    got = jnp.concatenate(
        [mm(eye(128), got[:, 128 * n : 128 * n + 128], NT) for n in range(5)], axis=0
    )
    qkv, proj = total[0:12, 0:288], total[0:12, 288:384]
    up = total[12:24, 0:384]
    down = [
        total[0:12, 384:480],
        total[12:24, 384:480],
        total[0:12, 480:576],
        total[12:24, 480:576],
    ]
    for z in range(Z):
        part = jnp.concatenate(
            [
                jnp.concatenate(
                    [qkv[:, 18 * z : 18 * z + 18], proj[:, 6 * z : 6 * z + 6]], axis=1
                ),
                up[:, 24 * z : 24 * z + 24],
                jnp.concatenate([piece[:, 6 * z : 6 * z + 6] for piece in down], axis=1),
            ],
            axis=0,
        )
        table = keep_ref[z, :, 0:69].astype(f32) + got[z * PER_Z : (z + 1) * PER_Z, 0:69]
        rest = jnp.concatenate(
            [
                jnp.concatenate([table[32:36, 23 * n : 23 * n + 23] for n in range(3)], axis=0),
                part[32:36, 0:23],
            ],
            axis=0,
        )
        rest = jnp.concatenate([rest, jnp.zeros((SEND - 16, 23), f32)], axis=0)
        last = jnp.concatenate([jnp.zeros((12, 1), f32), part[32:36, 23:24]], axis=0)
        last = jnp.concatenate([last, jnp.zeros((SEND - 16, 1), f32)], axis=0)
        out_ref[z] = jnp.concatenate(
            [table[0:SEND], part[0:SEND], rest, last, jnp.zeros((SEND, 11), f32)], axis=1
        ).astype(bf16)


def cells_kernel(own_ref, from_left_ref, from_right_ref, cells_ref, grad_ref):
    for which, ref in ((0, cells_ref), (1, grad_ref)):
        for level in range(LEVELS):
            lanes = slice(level * WIDTH, (level + 1) * WIDTH)
            own = own_ref[which, level].astype(f32)
            first, last = from_left_ref[which], from_right_ref[which]
            near, far = RIGHT * LAT, (WW - LEFT) * LAT
            ref[level] = jnp.concatenate(
                [
                    own[:near] + first.astype(f32)[:, lanes],
                    own[near:far],
                    own[far:] + last.astype(f32)[:, lanes],
                ],
                axis=0,
            ).astype(bf16)


def fin_kernel(scale, lat_ref, band_ref, in_ref, qkv_ref, proj_ref, up_ref, down_ref, route_ref):
    total = in_ref[0].astype(f32)
    for i in range(1, Z):
        total = total + in_ref[i].astype(f32)
    extra = jnp.concatenate([total[4 * n : 4 * n + 4, 93:116] for n in range(3)], axis=1)
    extra = jnp.concatenate([extra, total[12:16, 93:117], jnp.zeros((4, 35), f32)], axis=1)
    total = jnp.concatenate([total, extra], axis=0)
    qkv_ref[...] = total[0:12, 69:87] * scale
    proj_ref[...] = total[0:12, 87:93] * scale
    up_ref[...] = total[12:24, 69:93] * scale
    down_ref[...] = (
        jnp.concatenate([total[24:36, 69 + 6 * g : 75 + 6 * g] for g in range(4)], axis=0) * scale
    )
    table = total[0:36].astype(bf16)
    start, count = my_rows(lat_ref, band_ref)
    spot = line(NLAT * 32, 0)
    row, place = spot >> 4, spot & 15
    live = (row >= start) & (row < start + count) & (place < 9)
    wanted = jnp.where(live, (row - start) * 9 + place, -1)
    hits = one_hot(lax.broadcasted_iota(jnp.int32, (NLAT * 32, 36), 1) == wanted)
    route_ref[...] = mm(hits, table).reshape(NLAT, 32, 128).astype(bf16)


def table_kernel(in_ref, out_ref):
    total = in_ref[0].astype(f32)
    for i in range(1, NLAT):
        total = total + in_ref[i].astype(f32)
    for j in range(2):
        out_ref[j : j + 1, :] = jnp.concatenate(
            [total[j * 16 + n : j * 16 + n + 1, 0:69] for n in range(9)], axis=1
        )


def vmem():
    return pl.BlockSpec(memory_space=pltpu.VMEM)


def smem():
    return pl.BlockSpec(memory_space=pltpu.SMEM)


def params(mib):
    return pltpu.CompilerParams(vmem_limit_bytes=mib * 1024 * 1024)


def to_lon(x, by):
    count = lax.axis_size("lon")
    return lax.ppermute(x, "lon", [(i, (i + by) % count) for i in range(count)])


def prepare(lat, band_rows, bias_table, tables):
    return pl.pallas_call(
        prep_kernel,
        out_shape=jax.ShapeDtypeStruct((SLOTS, WTOK, ALL_Q), f32),
        in_specs=[smem()] * 2 + [vmem()] * 3,
        out_specs=vmem(),
        scratch_shapes=[pltpu.VMEM((8, HEADS * POS), f32), pltpu.VMEM((1152, HALF_V), f32)],
        compiler_params=params(24),
        cost_estimate=pl.CostEstimate(flops=1000000000, bytes_accessed=6000000, transcendentals=0),
        name="prepare",
    )(lat, band_rows, bias_table, *tables)


def early_part(lat, band_rows, lon_shift, own_t, own_c, w_qkv, w_proj, w_up, w_down_t):
    windows = jax.ShapeDtypeStruct((SLOTS, WTOK, WIDTH), f32)
    n_left, n_own, n_right = LEFT * LAT, WW * LAT, RIGHT * LAT
    shapes = ((288, n_left), (288, n_right), (n_left, 288), (n_own, 288), (n_right, 288))
    flips = ((3 * WIDTH, WIDTH), (WIDTH, WIDTH), (HID, WIDTH), (HID, WIDTH))
    flips = flips + ((288, 288), (288, 288))
    return pl.pallas_call(
        early_kernel,
        out_shape=(windows, windows)
        + tuple(jax.ShapeDtypeStruct(shape, bf16) for shape in shapes + flips),
        in_specs=[smem()] * 3 + [vmem()] * 6,
        out_specs=(vmem(),) * 13,
        compiler_params=params(24),
        cost_estimate=pl.CostEstimate(flops=1000000000, bytes_accessed=6000000, transcendentals=0),
        name="own_cells",
    )(lat, band_rows, lon_shift, own_t, own_c, w_qkv, w_proj, w_up, w_down_t)


def block_pass(half, left, right, early, bias, weights, tables):
    return pl.pallas_call(
        main_kernel,
        out_shape=(
            jax.ShapeDtypeStruct((2, LEFT * LAT, 2 * WIDTH), bf16),
            jax.ShapeDtypeStruct((2, LEVELS, WW * LAT, WIDTH), bf16),
            jax.ShapeDtypeStruct((2, RIGHT * LAT, 2 * WIDTH), bf16),
            jax.ShapeDtypeStruct((2 * NLAT, 112, 128), bf16),
            jax.ShapeDtypeStruct((Z, PER_Z, 128), bf16),
            jax.ShapeDtypeStruct((80, Z * PER_Z), bf16),
        ),
        in_specs=[smem()] + [vmem()] * 21,
        out_specs=(vmem(),) * 6,
        scratch_shapes=[
            pltpu.VMEM((SLOTS, WTOK, WIDTH), f32),
            pltpu.VMEM((SLOTS, WTOK, WIDTH), f32),
            pltpu.VMEM((SLOTS, WTOK, WIDTH), f32),
            pltpu.VMEM((SLOTS, WTOK, WIDTH), f32),
            pltpu.VMEM((SLOTS, WIDTH, ALL_Q), bf16),
            pltpu.VMEM((SLOTS, WIDTH, ALL_Q), bf16),
            pltpu.VMEM((WIDTH, 1536), f32),
            pltpu.VMEM((HID, WIDTH), f32),
            pltpu.VMEM((WIDTH, 768), f32),
            pltpu.VMEM((SLOTS, 288, 128), f32),
            pltpu.VMEM((NLON * PER_Z, 128), f32),
        ],
        compiler_params=params(32),
        name="block_pass",
    )(half, left, right, *early, bias, *weights, *tables)


def local(tokens, cotangent, w_qkv, w_proj, w_up, w_down, bias_table, band_rows, lon_shift):
    latwin = bias_table.shape[0]
    lat = lax.axis_index("lat").reshape(1)
    half = (lax.axis_index("lon") // Z).reshape(1)

    own_t = tokens.transpose(0, 2, 1, 3).reshape(LEVELS, WW * LAT, WIDTH)
    own_c = cotangent.transpose(0, 2, 1, 3).reshape(LEVELS, WW * LAT, WIDTH)
    spread, rows = make_tables()
    to_right, to_left = pl.pallas_call(
        pack_kernel,
        out_shape=(
            jax.ShapeDtypeStruct((2, LEFT * LAT, 2 * WIDTH), bf16),
            jax.ShapeDtypeStruct((2, RIGHT * LAT, 2 * WIDTH), bf16),
        ),
        in_specs=[pl.BlockSpec(memory_space=pl.ANY)] + [vmem()] * 2,
        out_specs=(vmem(),) * 2,
        compiler_params=params(16),
        name="pack_edges",
    )(rows, own_t, own_c)
    left = to_lon(to_right, 1)
    right = to_lon(to_left, -1)

    bias = prepare(lat, band_rows, bias_table, (rows, spread))
    w_down_t = w_down.T
    early = early_part(
        lat, band_rows, lon_shift, own_t, own_c, w_qkv, w_proj, w_up, w_down_t
    )
    flip = early[7:]
    weights = (w_qkv, flip[0], w_proj, flip[1], w_up, flip[2], flip[3], w_down_t)
    out_left, out_own, out_right, w_sums, t_keep, t_give = block_pass(
        half, left, right, early[:7], bias, weights, (spread, flip[4], flip[5])
    )

    t_got = to_lon(t_give, Z)
    from_right = to_lon(out_left, -1)
    from_left = to_lon(out_right, 1)
    near = [[(x * Z + z) * NLAT + i for x in range(2) for i in range(NLAT)] for z in range(Z)]
    ring = [[x * Z + z for z in range(Z)] for x in range(2)]
    w_got = lax.all_to_all(w_sums, ("lon", "lat"), 0, 0, axis_index_groups=near)
    cells_shape = jax.ShapeDtypeStruct((LEVELS, WW * LAT, WIDTH), bf16)
    lon_send = pl.pallas_call(
        mid_kernel,
        out_shape=jax.ShapeDtypeStruct((Z, SEND, 128), bf16),
        in_specs=[vmem()] * 3,
        out_specs=vmem(),
        compiler_params=params(24),
        name="sum_lat",
    )(w_got, t_keep, t_got)
    lon_send, from_left, from_right = lax.optimization_barrier(
        (lon_send, from_left, from_right)
    )
    cells, grads = pl.pallas_call(
        cells_kernel,
        out_shape=(cells_shape, cells_shape),
        in_specs=[vmem()] * 3,
        out_specs=(vmem(),) * 2,
        compiler_params=params(16),
        cost_estimate=pl.CostEstimate(flops=100000000, bytes_accessed=3000000, transcendentals=0),
        name="join_cells",
    )(out_own, from_left, from_right)
    output = cells.reshape(LEVELS, WW, LAT, WIDTH).transpose(0, 2, 1, 3)
    grad_tokens = grads.reshape(LEVELS, WW, LAT, WIDTH).transpose(0, 2, 1, 3)

    lon_got = lax.all_to_all(lon_send, "lon", 0, 0, axis_index_groups=ring)
    scale_grad = float(latwin * WH * LEVELS * WW * NLON) ** (-0.5)
    grad_qkv, grad_proj, grad_up, grad_down, route = pl.pallas_call(
        functools.partial(fin_kernel, scale_grad),
        out_shape=(
            jax.ShapeDtypeStruct((12, 18), f32),
            jax.ShapeDtypeStruct((12, 6), f32),
            jax.ShapeDtypeStruct((12, 24), f32),
            jax.ShapeDtypeStruct((48, 6), f32),
            jax.ShapeDtypeStruct((NLAT, 32, 128), bf16),
        ),
        in_specs=[smem(), smem(), vmem()],
        out_specs=(vmem(),) * 5,
        compiler_params=params(24),
        name="sum_lon",
    )(lat, band_rows, lon_got)
    route_got = lax.all_to_all(route, "lat", 0, 0)
    grad_table = pl.pallas_call(
        table_kernel,
        out_shape=jax.ShapeDtypeStruct((2, 621), f32),
        in_specs=[vmem()],
        out_specs=vmem(),
        compiler_params=params(24),
        name="sum_table",
    )(route_got)
    return (output, grad_tokens, grad_qkv, grad_proj, grad_up, grad_down, grad_table)


def solution(mesh):
    grid = P(None, "lat", "lon", None)
    cut = P("lat", "lon")
    return jax.shard_map(
        local,
        mesh=mesh,
        in_specs=(grid, grid, P(), P(), P(), P(), P(), P(), P()),
        out_specs=(grid, grid, cut, cut, cut, cut, cut),
        check_vma=False,
    )
```
